512 devices in a mesh: gr: 16 (over y, core), gc: 8 (over z), hd: 4 (over x).
Axes of the slice: x: 4, y: 8, z: 8, core: 2. Of those that a mesh axis runs over, the one named last changes fastest.
Arguments:
- patches: bfloat16 [128, 64, 1024], P('gr', 'gc', 'hd'), may hold values from -6 to 6
- w_in: bfloat16 [1024, 2, 1024], P(None, None, 'hd'), may hold values from -0.1875 to 0.1875
- w_bc: bfloat16 [1024, 4, 64], replicated, may hold values from -0.0625 to 0.0625
- w_step: bfloat16 [1024, 2, 16], P(None, None, 'hd'), may hold values from -0.1875 to 0.1875
- step_bias: float32 [2, 16], P(None, 'hd'), may hold values from -3 to 0.5
- decay_rate: float32 [2, 16], P(None, 'hd'), may hold values from 0.004 to 0.08
- skip_gain: float32 [16], P('hd'), may hold values from 0.25 to 2
- norm_gain: float32 [1024], P('hd'), may hold values from 0.25 to 1.75
- w_out: bfloat16 [1024, 1024], P('hd'), may hold values from -0.25 to 0.25
Outputs:
- mixed: bfloat16 [128, 64, 1024], P('gr', 'gc', 'hd')
The draws below stay inside these ranges and needn't reach their ends.
All inputs are finite; a program needn't handle non-finite values.
Results may differ from the reference program's by a relative error of at most 0.0049.
Values may be sent and summed in bfloat16 or wider, within the bound.
A program may use at most 64 MiB of HBM per device.

```python
import math
import jax
import jax.numpy as jnp
from jax import lax

D = 1024
NH = 16
NST = 64
E = 1024
HROWS = 128
WCOLS = 64


def with_spikes(drawn, stream_key, source, target, shards_of, factor):
    def block_of(dim):
        return (jnp.arange(drawn.shape[dim]) // (drawn.shape[dim] // shards_of)).reshape((-1,) + (1,) * (drawn.ndim - 1 - dim))

    near = jax.random.permutation(stream_key, shards_of)[block_of(target)]
    other_side = (block_of(target) + shards_of // 2) % shards_of
    return jnp.where((block_of(source) == near) | (block_of(source) == other_side), factor * drawn, drawn)


def shard_levels(own_key, shape, cuts, smallest, high):
    factor_of = 1.0
    for axis_at, parts in cuts:
        steps = jax.random.uniform(jax.random.fold_in(jax.random.fold_in(own_key, 6), axis_at), (parts,), jnp.float32, smallest / len(cuts), high / len(cuts))
        factor_of = factor_of * jnp.repeat(jnp.exp(steps), shape[axis_at] // parts).reshape((-1,) + (1,) * (len(shape) - 1 - axis_at))
    return factor_of


def gaussian(key, shape, deviation, limit, split=(), dtype=jnp.bfloat16):
    result = jax.random.normal(key, shape, jnp.float32) * deviation
    if len(split) > 0:
        result = shard_levels(key, shape, split, -0.22, 0.18) * result
    return jnp.clip(result, min=-limit, max=limit).astype(dtype)


def gaussian_with(key, extent, deviation, most, split, heavy, dtype=jnp.bfloat16):
    values = deviation * jax.random.normal(key, extent, jnp.float32)
    if split:
        values = values * shard_levels(key, extent, split, -0.22, 0.18)
    return jnp.clip(with_spikes(values, jax.random.fold_in(key, 3), *heavy), -most, most).astype(dtype)


def setup_inputs(seed: int = 0) -> dict:
    key_list = jax.random.split(jax.random.key(seed), 10)
    patches = gaussian(key_list[0], (HROWS, WCOLS, D), 1.0, 6.0, ((0, 16), (1, 8), (2, 4)))
    w_in = gaussian(key_list[1], (D, 2, E), D ** -0.5, 0.1875, ((2, 4),))
    w_bc = gaussian(key_list[2], (D, 4, NST), (D * 8) ** -0.5, 0.0625)
    w_step = gaussian(key_list[3], (D, 2, NH), D ** -0.5, 0.1875, ((2, 4),))
    step_bias = jnp.clip(-3.0 + 3.5 * jax.random.uniform(key_list[4], (2, NH), jnp.float32) ** shard_levels(key_list[4], (2, NH), ((1, 4),), -0.2, 0.2), -3.0, 0.5)
    decay_rate = jnp.clip(jnp.exp(math.log(0.08) - 2.9957322 * jax.random.uniform(key_list[5], (2, NH), jnp.float32) ** shard_levels(key_list[5], (2, NH), ((1, 4),), -0.2, 0.2)), 0.004, 0.08)
    skip_gain = jnp.clip(0.25 + 1.75 * jax.random.uniform(key_list[6], (NH,), jnp.float32) ** shard_levels(key_list[6], (NH,), ((0, 4),), -0.2, 0.2), 0.25, 2.0)
    norm_gain = jnp.clip(1.0 + 0.15 * jax.random.normal(key_list[7], (E,), jnp.float32), 0.25, 1.75)
    w_out = gaussian_with(key_list[8], (E, D), E ** -0.5, 0.25, ((0, 4),), (0, 1, 4, 2.0))
    return dict(patches=patches, w_in=w_in, w_bc=w_bc, w_step=w_step, step_bias=step_bias, decay_rate=decay_rate, skip_gain=skip_gain, norm_gain=norm_gain, w_out=w_out)


def directed_scan(rates, bmat, cmat, inputs):

    def advance(state, item):
        rate, bvec, cvec, xin = item
        state = jnp.exp(rate)[:, :, None, None] * state + bvec[:, None, :, None] * xin[:, :, None, :]
        out = jnp.einsum('an,ahnp->ahp', cvec, state, precision=lax.Precision.HIGHEST)
        return (state, out)
    lanes, _, heads, hsize = inputs.shape
    start = jnp.zeros((lanes, heads, bmat.shape[2], hsize), jnp.float32)
    items = (jnp.moveaxis(rates, 1, 0), jnp.moveaxis(bmat, 1, 0), jnp.moveaxis(cmat, 1, 0), jnp.moveaxis(inputs, 1, 0))
    _, outs = lax.scan(advance, start, items)
    return jnp.moveaxis(outs, 0, 1)

def reference(patches, w_in, w_bc, w_step, step_bias, decay_rate, skip_gain, norm_gain, w_out):
    rows, cols, width = patches.shape
    heads = w_step.shape[2]
    inner_width = w_in.shape[2]
    hsize = inner_width // heads
    flat = patches.reshape(rows * cols, width)
    inner = jnp.dot(flat, w_in.reshape(width, 2 * inner_width), preferred_element_type=jnp.float32)
    inner = inner.reshape(rows, cols, 2, heads, hsize)
    uvals = inner[:, :, 0]
    gate = inner[:, :, 1]
    bc = jnp.dot(flat, w_bc.reshape(width, -1), preferred_element_type=jnp.float32).reshape(rows, cols, 4, -1)
    raw = jnp.dot(flat, w_step.reshape(width, 2 * heads), preferred_element_type=jnp.float32).reshape(rows, cols, 2, heads)
    steps = jax.nn.softplus(raw + step_bias)
    rates = -decay_rate * steps
    horiz = directed_scan(rates[:, :, 0], bc[:, :, 0], bc[:, :, 1], steps[:, :, 0, :, None] * uvals)
    yh = horiz + skip_gain[:, None] * uvals
    vin = (steps[:, :, 1, :, None] * yh).transpose(1, 0, 2, 3)
    vert = directed_scan(rates[:, :, 1].transpose(1, 0, 2), bc[:, :, 2].transpose(1, 0, 2), bc[:, :, 3].transpose(1, 0, 2), vin)
    yv = vert.transpose(1, 0, 2, 3) + yh
    meansq = lax.optimization_barrier(jnp.mean(yv * yv, axis=-1, keepdims=True))
    normed = yv * lax.rsqrt(meansq + 1e-05) * norm_gain.reshape(heads, hsize)
    hidden = (normed * jax.nn.silu(gate)).astype(jnp.bfloat16).reshape(rows * cols, inner_width)
    mixed = jnp.dot(hidden, w_out, preferred_element_type=jnp.float32)
    return mixed.reshape(rows, cols, width).astype(jnp.bfloat16)
```

```python
import functools

import jax
import jax.numpy as jnp
from jax import lax
from jax.experimental import pallas as pl
from jax.experimental.pallas import tpu as pltpu
from jax.sharding import PartitionSpec as P

MESH = pl.DeviceIdType.MESH
F32, BF16 = jnp.float32, jnp.bfloat16
FAR_FIRST_8 = (4, 3, 5, 2, 6, 1, 7)
FAR_FIRST_4 = (2, 1, 3)


def nn(a, b):
    return lax.dot_general(a, b, (((1,), (0,)), ((), ())), preferred_element_type=F32)


def nt(a, b):
    return lax.dot_general(a, b, (((1,), (1,)), ((), ())), preferred_element_type=F32)


def split(a):
    high = a.astype(BF16)
    return high, (a - high.astype(F32)).astype(BF16)


def iotas(shape):
    return lax.broadcasted_iota(jnp.int32, shape, 0), lax.broadcasted_iota(jnp.int32, shape, 1)


def by_head(values, shape):
    lane = lax.broadcasted_iota(jnp.int32, shape, 1)
    row = jnp.full(shape, values[-1], F32)
    for h in range(len(values) - 2, -1, -1):
        row = jnp.where(lane < 64 * (h + 1), values[h], row)
    return row


def dots(c, b, copies):
    (c_high, c_low), (b_high, b_low) = split(c), split(b)
    lane = iotas(c.shape)[1]
    zero = jnp.zeros((), BF16)
    left = [jnp.where(lane < 64, c_high, c_low), jnp.where(lane < 64, c_high, zero)]
    right = jnp.concatenate([b_high, jnp.where(lane < 64, b_low, zero)], axis=1)
    return nt(jnp.concatenate(left, axis=1), jnp.concatenate([right] * copies, axis=0))


def segment_sums(rates, length, heads):
    k, lane = iotas((length, heads * length))
    inside = jnp.where(k > lane % length, rates, 0.0)
    high, low = split(inside)
    i, j = iotas((length, 2 * length))
    lower = jnp.where(i >= j % length, 1.0, 0.0).astype(BF16)
    return nn(lower, jnp.concatenate([high, low], axis=0))


def layer(
    patches, w_in, w_bc, w_step, bias_in, decay_in, skip_in, gain_in, w_out, out,
    pt, zs, zb, xr, xt, wi, wd, wb, wst, wh, wv, woc, gain, bias, decay, skip,
    yhz, yhb, es, eb, ys, yb, hs, hb, hx, ot, mix,
    load_sem, send_sem, recv_sem,
):
    gr, gc, hd = lax.axis_index("gr"), lax.axis_index("gc"), lax.axis_index("hd")
    chip, core = lax.div(gr, 2), lax.rem(gr, 2)

    x_peers = [lax.rem(hd + k, 4) for k in FAR_FIRST_4]
    z_peers = [lax.rem(gc + k, 8) for k in FAR_FIRST_8]
    y_peers = [2 * lax.rem(chip + k, 8) + c for k in FAR_FIRST_8 for c in (core, 1 - core)]
    y_peers.append(2 * chip + 1 - core)

    barrier = pltpu.get_barrier_semaphore()
    for p in z_peers:
        pl.semaphore_signal(barrier, inc=1, device_id=(gr, p, hd), device_id_type=MESH)
    for p in y_peers:
        pl.semaphore_signal(barrier, inc=1, device_id=(p, gc, hd), device_id_type=MESH)
    for p in x_peers:
        pl.semaphore_signal(barrier, inc=1, device_id=(gr, gc, p), device_id_type=MESH)

    def columns(p):
        return w_out.at[:, pl.ds(pl.multiple_of(p * 256, 256), 256)]

    loads = [
        pltpu.make_async_copy(src, dst, load_sem.at[n])
        for n, (src, dst) in enumerate(
            (
                (patches, pt),
                (w_step, wst),
                (w_bc, wb),
                (w_in, wi),
                (bias_in, bias),
                (decay_in, decay),
                (skip_in, skip),
                (gain_in, gain),
                (columns(hd), woc.at[hd]),
            )
        )
    ]
    for load in loads:
        load.start()

    def send(phase, src, dst, device):
        pltpu.make_async_remote_copy(
            src_ref=src,
            dst_ref=dst,
            send_sem=send_sem.at[phase],
            recv_sem=recv_sem.at[phase],
            device_id=device,
            device_id_type=MESH,
        ).start()

    def whole(phase, buf):
        part = buf.at[:, pl.ds(0, 56), :] if phase == 4 else buf.at[pl.ds(0, buf.shape[0] - 1)]
        return pltpu.make_async_remote_copy(
            src_ref=part,
            dst_ref=part,
            send_sem=send_sem.at[phase],
            recv_sem=recv_sem.at[phase],
            device_id=(gr, gc, x_peers[0]),
            device_id_type=MESH,
        )

    loads[0].wait()
    tile = pt[...].astype(F32)
    for r in range(8):
        zs[r] = jnp.concatenate([tile[r, :, 0:128], tile[r, :, 128:256]], axis=0).astype(BF16)
        for half in range(2):
            ot[half, 8 * r : 8 * r + 8, :] = tile[r, :, 128 * half : 128 * half + 128]
    for c in range(0, 8, 2):
        for half in range(2):
            pair = [ot[half, pl.ds(c + d, 8, stride=8), :] for d in (0, 1)]
            xt[hd, 8 * c : 8 * c + 16, 128 * half : 128 * half + 128] = jnp.concatenate(
                pair, axis=0
            ).astype(BF16)
    zb[gc] = zs[gc]

    pl.semaphore_wait(barrier, 25)

    for p in z_peers:
        send(0, zs.at[p], zb.at[gc], (gr, p, hd))
    for p in x_peers:
        send(1, xt.at[hd], xt.at[hd], (gr, gc, p))

    for load in loads[1:]:
        load.wait()

    def pairs(n, carry):
        rows = pl.ds(pl.multiple_of(n * 16, 16), 16)
        both = jnp.swapaxes(wi[rows].astype(F32), 0, 1)
        wd[:, rows, :] = both.astype(BF16)
        return carry

    lax.fori_loop(0, 64, pairs, 0)
    for n in range(4):
        wh[64 * n : 64 * n + 64, :] = wb[64 * (n // 2) : 64 * (n // 2) + 64, :]
    steps = wst[...].astype(F32)
    for h in range(4):
        wh[256 + 64 * h : 320 + 64 * h, :] = jnp.broadcast_to(steps[0, h : h + 1, :], (64, 1024)).astype(BF16)
        wv[64 * h : 64 * h + 64, :] = jnp.broadcast_to(steps[1, h : h + 1, :], (64, 1024)).astype(BF16)

    whole(0, zb).wait_recv()
    row = zb[...].astype(F32)
    xr[hd] = jnp.concatenate(
        [row[:, 0:8, :].reshape(64, 128), row[:, 8:16, :].reshape(64, 128)], axis=1
    ).astype(BF16)
    for p in x_peers:
        send(2, xr.at[hd], xr.at[hd], (gr, gc, p))

    whole(1, xt).wait_recv()
    gate = jnp.zeros((64, 256), F32)
    bcv = jnp.zeros((64, 128), F32)
    raw = jnp.zeros((64, 256), F32)
    for f in range(4):
        part, at = xt[f], slice(256 * f, 256 * f + 256)
        gate = gate + nn(part, wd[1, at, :])
        bcv = bcv + nt(part, wb[128:256, at])
        raw = raw + nt(part, wv[:, at])
    vstep = jax.nn.softplus(raw + by_head([bias[1, h] for h in range(4)], (64, 256)))
    gate = jax.nn.silu(gate) * gain[...]
    for c in range(8):
        at = slice(8 * c, 8 * c + 8)
        for half in range(2):
            lanes = slice(128 * half, 128 * half + 128)
            es[2 * c + half, :, 0:128] = gate[at, lanes]
            es[2 * c + half, :, 128:256] = bcv[at, :]
            es[2 * c + half, :, 256:384] = vstep[at, lanes]
    eb[gr] = es[gr]
    for p in y_peers:
        send(3, es.at[p], eb.at[gr], (p, gc, hd))

    whole(2, xr).wait_recv()
    uvals = jnp.zeros((64, 256), F32)
    proj = jnp.zeros((64, 512), F32)
    for f in range(4):
        part, at = xr[f], slice(256 * f, 256 * f + 256)
        uvals = uvals + nn(part, wd[0, at, :])
        proj = proj + nt(part, wh[:, at])
    hstep = jax.nn.softplus(proj[:, 256:512] + by_head([bias[0, h] for h in range(4)], (64, 256)))
    sums = segment_sums(hstep * by_head([-decay[0, h] for h in range(4)], (64, 256)), 64, 4)
    scores = dots(proj[:, 128:256], proj[:, 0:128], 4)
    i, lane = iotas((64, 256))
    mixing = jnp.where(i >= lane % 64, scores * jnp.exp(sums), 0.0)
    k, lane = iotas((256, 256))
    x_high, x_low = (
        jnp.where(k // 64 == lane // 64, jnp.concatenate([part] * 4, axis=0), jnp.zeros((), BF16))
        for part in split(hstep * uvals)
    )
    high, low = split(mixing)
    yh = nn(high, x_high) + nn(low, x_high) + nn(high, x_low)
    yh = yh + uvals * by_head([skip[h] for h in range(4)], (64, 256))
    def eight(n):
        return pl.ds(pl.multiple_of(n * 8, 8), 8)

    for half in range(2):
        yhz[half] = yh[:, 128 * half : 128 * half + 128]
        yhb[half, eight(gc), :] = yhz[half, eight(gc), :]
    for p in z_peers:
        send(4, yhz.at[:, eight(p), :], yhb.at[:, eight(gc), :], (gr, p, hd))

    for p in x_peers:
        send(5, columns(p), woc.at[hd], (gr, gc, p))

    whole(3, eb).wait_recv()
    ready = eb[...].reshape(128, 384)
    vdt = ready[:, 256:384]
    rates = jnp.concatenate(
        [
            jnp.broadcast_to(vdt[:, 64 * h : 64 * h + 1] * -decay[1, 2 * core + h], (128, 128))
            for h in range(2)
        ],
        axis=1,
    )
    sums = segment_sums(rates, 128, 2)
    bmat, cmat = (jnp.concatenate([ready[:, at : at + 64]] * 2, axis=1) for at in (128, 192))
    scores = dots(cmat, bmat, 2)
    i, lane = iotas((128, 256))
    high, low = split(jnp.where(i >= lane % 128, scores * jnp.exp(sums), 0.0))
    mix[:, 0:256] = high
    mix[:, 256:512] = low

    whole(4, yhb).wait_recv()
    for c in range(8):
        for half in range(2):
            ys[2 * c + half] = yhb[half, pl.ds(c, 8, stride=8), :]
    yb[gr] = ys[gr]
    for p in y_peers:
        send(6, ys.at[p], yb.at[gr], (p, gc, hd))

    whole(0, zb).wait_send()
    whole(1, xt).wait_send()
    whole(2, xr).wait_send()
    whole(3, eb).wait_send()
    whole(4, yhb).wait_send()
    whole(5, woc).wait_send()

    whole(6, yb).wait_recv()
    yh = yb[...].reshape(128, 128)
    k, lane = iotas((128, 128))
    zero = jnp.zeros((), BF16)
    x_high, x_low = (
        jnp.concatenate([jnp.where(lane < 64, part, zero), jnp.where(lane >= 64, part, zero)], axis=0)
        for part in split(eb[...].reshape(128, 384)[:, 256:384] * yh)
    )
    yv = nn(mix[:, 0:256], x_high) + nn(mix[:, 256:512], x_high) + nn(mix[:, 0:256], x_low) + yh
    high, low = split(yv * yv)
    k, lane = iotas((256, 128))
    same = jnp.where((k % 128) // 64 == lane // 64, 1.0, 0.0).astype(BF16)
    meansq = nn(jnp.concatenate([high, low], axis=1), same) * (1.0 / 64.0)
    hidden = yv * lax.rsqrt(meansq + 1e-05) * eb[...].reshape(128, 384)[:, 0:128]
    hs[...] = hidden.astype(BF16).astype(F32).reshape(16, 8, 128)
    hb[gr] = hs[gr]
    for p in y_peers:
        send(7, hs.at[p], hb.at[gr], (p, gc, hd))
    whole(6, yb).wait_send()

    whole(7, hb).wait_recv()
    for c in range(8):
        for half in range(2):
            ot[half, pl.ds(c, 8, stride=8), :] = hb[2 * c + half]
    hx[hd] = jnp.concatenate([ot[0], ot[1]], axis=1).astype(BF16)
    for p in x_peers:
        send(8, hx.at[hd], hx.at[hd], (gr, gc, p))
    whole(7, hb).wait_send()
    whole(5, woc).wait_recv()
    whole(8, hx).wait_recv()
    mixed = jnp.zeros((64, 256), F32)
    for f in range(4):
        mixed = mixed + nn(hx[f], woc[f])
    out[...] = mixed.astype(BF16)
    whole(8, hx).wait_send()


def on_device(patches, w_in, w_bc, w_step, step_bias, decay_rate, skip_gain, norm_gain, w_out):
    hbm, vmem, smem = (pl.BlockSpec(memory_space=m) for m in (pltpu.HBM, pltpu.VMEM, pltpu.SMEM))
    scratch = [
        pltpu.VMEM((8, 8, 256), BF16),
        pltpu.VMEM((8, 16, 128), BF16),
        pltpu.VMEM((8, 16, 128), BF16),
        pltpu.VMEM((4, 64, 256), BF16),
        pltpu.VMEM((4, 64, 256), BF16),
        pltpu.VMEM((1024, 2, 256), BF16),
        pltpu.VMEM((2, 1024, 256), BF16),
        pltpu.VMEM((256, 1024), BF16),
        pltpu.VMEM((2, 4, 1024), BF16),
        pltpu.VMEM((512, 1024), BF16),
        pltpu.VMEM((256, 1024), BF16),
        pltpu.VMEM((4, 256, 256), BF16),
        pltpu.VMEM((1, 256), F32),
        pltpu.SMEM((2, 4), F32),
        pltpu.SMEM((2, 4), F32),
        pltpu.SMEM((4,), F32),
        pltpu.VMEM((2, 64, 128), F32),
        pltpu.VMEM((2, 64, 128), F32),
        pltpu.VMEM((16, 8, 384), F32),
        pltpu.VMEM((16, 8, 384), F32),
        pltpu.VMEM((16, 8, 128), F32),
        pltpu.VMEM((16, 8, 128), F32),
        pltpu.VMEM((16, 8, 128), F32),
        pltpu.VMEM((16, 8, 128), F32),
        pltpu.VMEM((4, 64, 256), BF16),
        pltpu.VMEM((2, 64, 128), F32),
        pltpu.VMEM((128, 512), BF16),
        pltpu.SemaphoreType.DMA((9,)),
        pltpu.SemaphoreType.DMA((9,)),
        pltpu.SemaphoreType.DMA((9,)),
    ]
    mixed = pl.pallas_call(
        layer,
        out_shape=jax.ShapeDtypeStruct((64, 256), BF16),
        in_specs=[hbm] * 9,
        out_specs=vmem,
        scratch_shapes=scratch,
        compiler_params=pltpu.CompilerParams(
            collective_id=0, has_side_effects=True, vmem_limit_bytes=60 * 2**20
        ),
    )(
        patches,
        w_in,
        w_bc.transpose(1, 2, 0).reshape(256, 1024),
        w_step.transpose(1, 2, 0),
        step_bias,
        decay_rate,
        skip_gain,
        norm_gain.reshape(1, 256),
        w_out,
    )
    return mixed.reshape(8, 8, 256)


def solution(mesh):
    in_specs = (
        P("gr", "gc", "hd"),
        P(None, None, "hd"),
        P(),
        P(None, None, "hd"),
        P(None, "hd"),
        P(None, "hd"),
        P("hd"),
        P("hd"),
        P("hd", None),
    )
    out_specs = P("gr", "gc", "hd")
    return jax.shard_map(
        on_device, mesh=mesh, in_specs=in_specs, out_specs=out_specs, check_vma=False
    )
```

```python
import functools

import jax
import jax.numpy as jnp
from jax import lax
from jax.experimental import pallas as pl
from jax.experimental.pallas import tpu as pltpu
from jax.sharding import PartitionSpec as P

MESH = pl.DeviceIdType.MESH
F32, BF16 = jnp.float32, jnp.bfloat16
FAR_FIRST_8 = (4, 3, 5, 2, 6, 1, 7)
FAR_FIRST_4 = (2, 1, 3)


def nn(a, b):
    return lax.dot_general(a, b, (((1,), (0,)), ((), ())), preferred_element_type=F32)


def nt(a, b):
    return lax.dot_general(a, b, (((1,), (1,)), ((), ())), preferred_element_type=F32)


def split(a):
    high = a.astype(BF16)
    return high, (a - high.astype(F32)).astype(BF16)


def iotas(shape):
    return lax.broadcasted_iota(jnp.int32, shape, 0), lax.broadcasted_iota(jnp.int32, shape, 1)


def by_head(values, shape):
    lane = lax.broadcasted_iota(jnp.int32, shape, 1)
    row = jnp.full(shape, values[-1], F32)
    for h in range(len(values) - 2, -1, -1):
        row = jnp.where(lane < 64 * (h + 1), values[h], row)
    return row


def dots(c, b, copies):
    (c_high, c_low), (b_high, b_low) = split(c), split(b)
    lane = iotas(c.shape)[1]
    zero = jnp.zeros((), BF16)
    left = [jnp.where(lane < 64, c_high, c_low), jnp.where(lane < 64, c_high, zero)]
    right = jnp.concatenate([b_high, jnp.where(lane < 64, b_low, zero)], axis=1)
    return nt(jnp.concatenate(left, axis=1), jnp.concatenate([right] * copies, axis=0))


def segment_sums(rates, length, heads):
    k, lane = iotas((length, heads * length))
    inside = jnp.where(k > lane % length, rates, 0.0)
    high, low = split(inside)
    i, j = iotas((length, 2 * length))
    lower = jnp.where(i >= j % length, 1.0, 0.0).astype(BF16)
    return nn(lower, jnp.concatenate([high, low], axis=0))


def layer(
    patches, w_in, w_bc, w_step, bias_in, decay_in, skip_in, gain_in, w_out, out,
    pt, zs, zb, xr, xt, wi, wd, wb, wst, wh, wv, woc, gain, bias, decay, skip,
    yhz, yhb, es, eb, ys, yb, hs, hx, ot, mix,
    load_sem, send_sem, recv_sem,
):
    gr, gc, hd = lax.axis_index("gr"), lax.axis_index("gc"), lax.axis_index("hd")
    chip, core = lax.div(gr, 2), lax.rem(gr, 2)

    x_peers = [lax.rem(hd + k, 4) for k in FAR_FIRST_4]
    z_peers = [lax.rem(gc + k, 8) for k in FAR_FIRST_8]
    y_peers = [2 * lax.rem(chip + k, 8) + c for k in FAR_FIRST_8 for c in (core, 1 - core)]
    y_peers.append(2 * chip + 1 - core)

    barrier = pltpu.get_barrier_semaphore()
    for p in z_peers:
        pl.semaphore_signal(barrier, inc=1, device_id=(gr, p, hd), device_id_type=MESH)
    for p in y_peers:
        pl.semaphore_signal(barrier, inc=1, device_id=(p, gc, hd), device_id_type=MESH)
    for p in x_peers:
        pl.semaphore_signal(barrier, inc=1, device_id=(gr, gc, p), device_id_type=MESH)

    def columns(p):
        return w_out.at[:, pl.ds(pl.multiple_of(p * 256, 256), 256)]

    loads = [
        pltpu.make_async_copy(src, dst, load_sem.at[n])
        for n, (src, dst) in enumerate(
            (
                (patches, pt),
                (w_step, wst),
                (w_bc, wb),
                (w_in, wi),
                (bias_in, bias),
                (decay_in, decay),
                (skip_in, skip),
                (gain_in, gain),
                (columns(hd), woc.at[hd]),
            )
        )
    ]
    for load in loads:
        load.start()

    def send(phase, src, dst, device):
        pltpu.make_async_remote_copy(
            src_ref=src,
            dst_ref=dst,
            send_sem=send_sem.at[phase],
            recv_sem=recv_sem.at[phase],
            device_id=device,
            device_id_type=MESH,
        ).start()

    def whole(phase, buf):
        part = buf.at[:, pl.ds(0, 56), :] if phase == 4 else buf.at[pl.ds(0, buf.shape[0] - 1)]
        return pltpu.make_async_remote_copy(
            src_ref=part,
            dst_ref=part,
            send_sem=send_sem.at[phase],
            recv_sem=recv_sem.at[phase],
            device_id=(gr, gc, x_peers[0]),
            device_id_type=MESH,
        )

    loads[0].wait()
    tile = pt[...].astype(F32)
    for r in range(8):
        zs[r] = jnp.concatenate([tile[r, :, 0:128], tile[r, :, 128:256]], axis=0).astype(BF16)
        for half in range(2):
            ot[half, 8 * r : 8 * r + 8, :] = tile[r, :, 128 * half : 128 * half + 128]
    for c in range(0, 8, 2):
        for half in range(2):
            pair = [ot[half, pl.ds(c + d, 8, stride=8), :] for d in (0, 1)]
            xt[hd, 8 * c : 8 * c + 16, 128 * half : 128 * half + 128] = jnp.concatenate(
                pair, axis=0
            ).astype(BF16)
    zb[gc] = zs[gc]

    pl.semaphore_wait(barrier, 25)

    for p in z_peers:
        send(0, zs.at[p], zb.at[gc], (gr, p, hd))
    for p in x_peers:
        send(1, xt.at[hd], xt.at[hd], (gr, gc, p))

    for load in loads[1:]:
        load.wait()

    def pairs(n, carry):
        rows = pl.ds(pl.multiple_of(n * 16, 16), 16)
        both = jnp.swapaxes(wi[rows].astype(F32), 0, 1)
        wd[:, rows, :] = both.astype(BF16)
        return carry

    lax.fori_loop(0, 64, pairs, 0)
    for n in range(4):
        wh[64 * n : 64 * n + 64, :] = wb[64 * (n // 2) : 64 * (n // 2) + 64, :]
    steps = wst[...].astype(F32)
    for h in range(4):
        wh[256 + 64 * h : 320 + 64 * h, :] = jnp.broadcast_to(steps[0, h : h + 1, :], (64, 1024)).astype(BF16)
        wv[64 * h : 64 * h + 64, :] = jnp.broadcast_to(steps[1, h : h + 1, :], (64, 1024)).astype(BF16)

    whole(0, zb).wait_recv()
    row = zb[...].astype(F32)
    xr[hd] = jnp.concatenate(
        [row[:, 0:8, :].reshape(64, 128), row[:, 8:16, :].reshape(64, 128)], axis=1
    ).astype(BF16)
    for p in x_peers:
        send(2, xr.at[hd], xr.at[hd], (gr, gc, p))

    whole(1, xt).wait_recv()
    gate = jnp.zeros((64, 256), F32)
    bcv = jnp.zeros((64, 128), F32)
    raw = jnp.zeros((64, 256), F32)
    for f in range(4):
        part, at = xt[f], slice(256 * f, 256 * f + 256)
        gate = gate + nn(part, wd[1, at, :])
        bcv = bcv + nt(part, wb[128:256, at])
        raw = raw + nt(part, wv[:, at])
    vstep = jax.nn.softplus(raw + by_head([bias[1, h] for h in range(4)], (64, 256)))
    gate = jax.nn.silu(gate) * gain[...]
    for c in range(8):
        at = slice(8 * c, 8 * c + 8)
        for half in range(2):
            lanes = slice(128 * half, 128 * half + 128)
            es[2 * c + half, :, 0:128] = gate[at, lanes]
            es[2 * c + half, :, 128:256] = bcv[at, :]
            es[2 * c + half, :, 256:384] = vstep[at, lanes]
    eb[gr] = es[gr]
    for p in y_peers:
        send(3, es.at[p], eb.at[gr], (p, gc, hd))

    whole(2, xr).wait_recv()
    uvals = jnp.zeros((64, 256), F32)
    proj = jnp.zeros((64, 512), F32)
    for f in range(4):
        part, at = xr[f], slice(256 * f, 256 * f + 256)
        uvals = uvals + nn(part, wd[0, at, :])
        proj = proj + nt(part, wh[:, at])
    hstep = jax.nn.softplus(proj[:, 256:512] + by_head([bias[0, h] for h in range(4)], (64, 256)))
    sums = segment_sums(hstep * by_head([-decay[0, h] for h in range(4)], (64, 256)), 64, 4)
    scores = dots(proj[:, 128:256], proj[:, 0:128], 4)
    i, lane = iotas((64, 256))
    mixing = jnp.where(i >= lane % 64, scores * jnp.exp(sums), 0.0)
    k, lane = iotas((256, 256))
    x_high, x_low = (
        jnp.where(k // 64 == lane // 64, jnp.concatenate([part] * 4, axis=0), jnp.zeros((), BF16))
        for part in split(hstep * uvals)
    )
    high, low = split(mixing)
    yh = nn(high, x_high) + nn(low, x_high) + nn(high, x_low)
    yh = yh + uvals * by_head([skip[h] for h in range(4)], (64, 256))
    def eight(n):
        return pl.ds(pl.multiple_of(n * 8, 8), 8)

    for half in range(2):
        yhz[half] = yh[:, 128 * half : 128 * half + 128]
        yhb[half, eight(gc), :] = yhz[half, eight(gc), :]
    for p in z_peers:
        send(4, yhz.at[:, eight(p), :], yhb.at[:, eight(gc), :], (gr, p, hd))

    for p in x_peers:
        send(5, columns(p), woc.at[hd], (gr, gc, p))

    whole(3, eb).wait_recv()
    ready = eb[...].reshape(128, 384)
    vdt = ready[:, 256:384]
    rates = jnp.concatenate(
        [
            jnp.broadcast_to(vdt[:, 64 * h : 64 * h + 1] * -decay[1, 2 * core + h], (128, 128))
            for h in range(2)
        ],
        axis=1,
    )
    sums = segment_sums(rates, 128, 2)
    bmat, cmat = (jnp.concatenate([ready[:, at : at + 64]] * 2, axis=1) for at in (128, 192))
    scores = dots(cmat, bmat, 2)
    i, lane = iotas((128, 256))
    high, low = split(jnp.where(i >= lane % 128, scores * jnp.exp(sums), 0.0))
    mix[:, 0:256] = high
    mix[:, 256:512] = low

    whole(4, yhb).wait_recv()
    for c in range(8):
        for half in range(2):
            ys[2 * c + half] = yhb[half, pl.ds(c, 8, stride=8), :]
    yb[gr] = ys[gr]
    for p in y_peers:
        send(6, ys.at[p], yb.at[gr], (p, gc, hd))

    whole(0, zb).wait_send()
    whole(1, xt).wait_send()
    whole(2, xr).wait_send()
    whole(3, eb).wait_send()
    whole(4, yhb).wait_send()
    whole(5, woc).wait_send()

    whole(6, yb).wait_recv()
    yh = yb[...].reshape(128, 128)
    k, lane = iotas((128, 128))
    zero = jnp.zeros((), BF16)
    x_high, x_low = (
        jnp.concatenate([jnp.where(lane < 64, part, zero), jnp.where(lane >= 64, part, zero)], axis=0)
        for part in split(eb[...].reshape(128, 384)[:, 256:384] * yh)
    )
    yv = nn(mix[:, 0:256], x_high) + nn(mix[:, 256:512], x_high) + nn(mix[:, 0:256], x_low) + yh
    high, low = split(yv * yv)
    k, lane = iotas((256, 128))
    same = jnp.where((k % 128) // 64 == lane // 64, 1.0, 0.0).astype(BF16)
    meansq = nn(jnp.concatenate([high, low], axis=1), same) * (1.0 / 64.0)
    hidden = yv * lax.rsqrt(meansq + 1e-05) * eb[...].reshape(128, 384)[:, 0:128]
    hs[...] = hidden.reshape(16, 8, 128).astype(BF16)

    slot = (2 * hd + core) * 8 + chip
    hx[slot] = hs[gr]
    for p in y_peers + [gr]:
        for q in x_peers + [hd]:
            if not (p is gr and q is hd):
                send(7, hs.at[p], hx.at[slot], (p, gc, q))
    whole(6, yb).wait_send()
    whole(5, woc).wait_recv()

    whole(7, hx).wait_recv()
    mixed = jnp.zeros((64, 256), F32)
    for f in range(4):
        part = [hx[at : at + 8].astype(F32).reshape(64, 128) for at in (16 * f, 16 * f + 8)]
        mixed = mixed + nn(jnp.concatenate(part, axis=1).astype(BF16), woc[f])
    for c in range(8):
        for half in range(2):
            ot[half, pl.ds(c, 8, stride=8), :] = mixed[8 * c : 8 * c + 8, 128 * half : 128 * half + 128]
    out[...] = jnp.concatenate([ot[0], ot[1]], axis=1).astype(BF16)
    whole(7, hx).wait_send()


def on_device(patches, w_in, w_bc, w_step, step_bias, decay_rate, skip_gain, norm_gain, w_out):
    hbm, vmem, smem = (pl.BlockSpec(memory_space=m) for m in (pltpu.HBM, pltpu.VMEM, pltpu.SMEM))
    scratch = [
        pltpu.VMEM((8, 8, 256), BF16),
        pltpu.VMEM((8, 16, 128), BF16),
        pltpu.VMEM((8, 16, 128), BF16),
        pltpu.VMEM((4, 64, 256), BF16),
        pltpu.VMEM((4, 64, 256), BF16),
        pltpu.VMEM((1024, 2, 256), BF16),
        pltpu.VMEM((2, 1024, 256), BF16),
        pltpu.VMEM((256, 1024), BF16),
        pltpu.VMEM((2, 4, 1024), BF16),
        pltpu.VMEM((512, 1024), BF16),
        pltpu.VMEM((256, 1024), BF16),
        pltpu.VMEM((4, 256, 256), BF16),
        pltpu.VMEM((1, 256), F32),
        pltpu.SMEM((2, 4), F32),
        pltpu.SMEM((2, 4), F32),
        pltpu.SMEM((4,), F32),
        pltpu.VMEM((2, 64, 128), F32),
        pltpu.VMEM((2, 64, 128), F32),
        pltpu.VMEM((16, 8, 384), F32),
        pltpu.VMEM((16, 8, 384), F32),
        pltpu.VMEM((16, 8, 128), F32),
        pltpu.VMEM((16, 8, 128), F32),
        pltpu.VMEM((16, 8, 128), BF16),
        pltpu.VMEM((64, 8, 128), BF16),
        pltpu.VMEM((2, 64, 128), F32),
        pltpu.VMEM((128, 512), BF16),
        pltpu.SemaphoreType.DMA((9,)),
        pltpu.SemaphoreType.DMA((8,)),
        pltpu.SemaphoreType.DMA((8,)),
    ]
    mixed = pl.pallas_call(
        layer,
        out_shape=jax.ShapeDtypeStruct((64, 256), BF16),
        in_specs=[hbm] * 9,
        out_specs=vmem,
        scratch_shapes=scratch,
        compiler_params=pltpu.CompilerParams(
            collective_id=0, has_side_effects=True, vmem_limit_bytes=60 * 2**20
        ),
    )(
        patches,
        w_in,
        w_bc.transpose(1, 2, 0).reshape(256, 1024),
        w_step.transpose(1, 2, 0),
        step_bias,
        decay_rate,
        skip_gain,
        norm_gain.reshape(1, 256),
        w_out,
    )
    return mixed.reshape(8, 8, 256)


def solution(mesh):
    in_specs = (
        P("gr", "gc", "hd"),
        P(None, None, "hd"),
        P(),
        P(None, None, "hd"),
        P(None, "hd"),
        P(None, "hd"),
        P("hd"),
        P("hd"),
        P("hd", None),
    )
    out_specs = P("gr", "gc", "hd")
    return jax.shard_map(
        on_device, mesh=mesh, in_specs=in_specs, out_specs=out_specs, check_vma=False
    )
```

```python
import functools

import jax
import jax.numpy as jnp
from jax import lax
from jax.experimental import pallas as pl
from jax.experimental.pallas import tpu as pltpu
from jax.sharding import PartitionSpec as P

MESH = pl.DeviceIdType.MESH
F32, BF16 = jnp.float32, jnp.bfloat16
FAR_FIRST_8 = (4, 3, 5, 2, 6, 1, 7)
FAR_FIRST_4 = (2, 1, 3)


def abs_hops(k):
    return min(k, 8 - k)


def nn(a, b):
    return lax.dot_general(a, b, (((1,), (0,)), ((), ())), preferred_element_type=F32)


def nt(a, b):
    return lax.dot_general(a, b, (((1,), (1,)), ((), ())), preferred_element_type=F32)


def split(a):
    high = a.astype(BF16)
    return high, (a - high.astype(F32)).astype(BF16)


def iotas(shape):
    return lax.broadcasted_iota(jnp.int32, shape, 0), lax.broadcasted_iota(jnp.int32, shape, 1)


def by_head(values, shape):
    lane = lax.broadcasted_iota(jnp.int32, shape, 1)
    row = jnp.full(shape, values[-1], F32)
    for h in range(len(values) - 2, -1, -1):
        row = jnp.where(lane < 64 * (h + 1), values[h], row)
    return row


def dots(c, b, copies):
    (c_high, c_low), (b_high, b_low) = split(c), split(b)
    lane = iotas(c.shape)[1]
    zero = jnp.zeros((), BF16)
    left = [jnp.where(lane < 64, c_high, c_low), jnp.where(lane < 64, c_high, zero)]
    right = jnp.concatenate([b_high, jnp.where(lane < 64, b_low, zero)], axis=1)
    return nt(jnp.concatenate(left, axis=1), jnp.concatenate([right] * copies, axis=0))


def segment_sums(rates, length, heads):
    k, lane = iotas((length, heads * length))
    inside = jnp.where(k > lane % length, rates, 0.0)
    high, low = split(inside)
    i, j = iotas((length, 2 * length))
    lower = jnp.where(i >= j % length, 1.0, 0.0).astype(BF16)
    return nn(lower, jnp.concatenate([high, low], axis=0))


def layer(
    patches, w_in, w_bc, w_step, bias_in, decay_in, skip_in, gain_in, w_out, out,
    pt, zs, zb, xr, xt, wi, wd, wb, wst, wh, wv, woc, gain, bias, decay, skip,
    yhz, es, eb, yb, hs, hx, ot, mix,
    load_sem, send_sem, recv_sem,
):
    gr, gc, hd = lax.axis_index("gr"), lax.axis_index("gc"), lax.axis_index("hd")
    chip, core = lax.div(gr, 2), lax.rem(gr, 2)

    x_peers = [lax.rem(hd + k, 4) for k in FAR_FIRST_4]
    z_peers = [lax.rem(gc + k, 8) for k in FAR_FIRST_8]
    y_peers = [2 * lax.rem(chip + k, 8) + c for k in FAR_FIRST_8 for c in (core, 1 - core)]
    y_peers.append(2 * chip + 1 - core)

    plane = [
        (far + abs_hops(k), p, q)
        for far, p in zip((4, 4, 3, 3, 3, 3, 2, 2, 2, 2, 1, 1, 1, 1, 0, 0), y_peers + [gr])
        for k, q in zip(FAR_FIRST_8 + (0,), z_peers + [gc])
    ]
    plane = [(p, q) for _, p, q in sorted(plane[:-1], key=lambda entry: -entry[0])]

    barrier = pltpu.get_barrier_semaphore()
    for p in z_peers:
        pl.semaphore_signal(barrier, inc=1, device_id=(gr, p, hd), device_id_type=MESH)
    for p in y_peers:
        pl.semaphore_signal(barrier, inc=1, device_id=(p, gc, hd), device_id_type=MESH)
    for p in x_peers:
        pl.semaphore_signal(barrier, inc=1, device_id=(gr, gc, p), device_id_type=MESH)

    def columns(p):
        return w_out.at[:, pl.ds(pl.multiple_of(p * 256, 256), 256)]

    loads = [
        pltpu.make_async_copy(src, dst, load_sem.at[n])
        for n, (src, dst) in enumerate(
            (
                (patches, pt),
                (w_step, wst),
                (w_bc, wb),
                (w_in, wi),
                (bias_in, bias),
                (decay_in, decay),
                (skip_in, skip),
                (gain_in, gain),
                (columns(hd), woc.at[hd]),
            )
        )
    ]
    for load in loads:
        load.start()

    def send(phase, src, dst, device):
        pltpu.make_async_remote_copy(
            src_ref=src,
            dst_ref=dst,
            send_sem=send_sem.at[phase],
            recv_sem=recv_sem.at[phase],
            device_id=device,
            device_id_type=MESH,
        ).start()

    def whole(phase, buf):
        part = buf.at[pl.ds(0, buf.shape[0] - 1)]
        return pltpu.make_async_remote_copy(
            src_ref=part,
            dst_ref=part,
            send_sem=send_sem.at[phase],
            recv_sem=recv_sem.at[phase],
            device_id=(gr, gc, x_peers[0]),
            device_id_type=MESH,
        )

    loads[0].wait()
    tile = pt[...].astype(F32)
    for r in range(8):
        zs[r] = jnp.concatenate([tile[r, :, 0:128], tile[r, :, 128:256]], axis=0).astype(BF16)
        for half in range(2):
            ot[half, 8 * r : 8 * r + 8, :] = tile[r, :, 128 * half : 128 * half + 128]
    for c in range(0, 8, 2):
        for half in range(2):
            pair = [ot[half, pl.ds(c + d, 8, stride=8), :] for d in (0, 1)]
            xt[hd, 8 * c : 8 * c + 16, 128 * half : 128 * half + 128] = jnp.concatenate(
                pair, axis=0
            ).astype(BF16)
    zb[gc] = zs[gc]

    pl.semaphore_wait(barrier, 25)

    for p in z_peers:
        send(0, zs.at[p], zb.at[gc], (gr, p, hd))
    for p in x_peers:
        send(1, xt.at[hd], xt.at[hd], (gr, gc, p))

    for load in loads[1:]:
        load.wait()

    def pairs(n, carry):
        rows = pl.ds(pl.multiple_of(n * 16, 16), 16)
        both = jnp.swapaxes(wi[rows].astype(F32), 0, 1)
        wd[:, rows, :] = both.astype(BF16)
        return carry

    lax.fori_loop(0, 64, pairs, 0)
    for n in range(4):
        wh[64 * n : 64 * n + 64, :] = wb[64 * (n // 2) : 64 * (n // 2) + 64, :]
    steps = wst[...].astype(F32)
    for h in range(4):
        wh[256 + 64 * h : 320 + 64 * h, :] = jnp.broadcast_to(steps[0, h : h + 1, :], (64, 1024)).astype(BF16)
        wv[64 * h : 64 * h + 64, :] = jnp.broadcast_to(steps[1, h : h + 1, :], (64, 1024)).astype(BF16)

    whole(0, zb).wait_recv()
    row = zb[...].astype(F32)
    xr[hd] = jnp.concatenate(
        [row[:, 0:8, :].reshape(64, 128), row[:, 8:16, :].reshape(64, 128)], axis=1
    ).astype(BF16)
    for p in x_peers:
        send(2, xr.at[hd], xr.at[hd], (gr, gc, p))

    whole(1, xt).wait_recv()
    gate = jnp.zeros((64, 256), F32)
    bcv = jnp.zeros((64, 128), F32)
    raw = jnp.zeros((64, 256), F32)
    for f in range(4):
        part, at = xt[f], slice(256 * f, 256 * f + 256)
        gate = gate + nn(part, wd[1, at, :])
        bcv = bcv + nt(part, wb[128:256, at])
        raw = raw + nt(part, wv[:, at])
    vstep = jax.nn.softplus(raw + by_head([bias[1, h] for h in range(4)], (64, 256)))
    gate = jax.nn.silu(gate) * gain[...]
    for c in range(8):
        at = slice(8 * c, 8 * c + 8)
        for half in range(2):
            lanes = slice(128 * half, 128 * half + 128)
            es[2 * c + half, :, 0:128] = gate[at, lanes]
            es[2 * c + half, :, 128:256] = bcv[at, :]
            es[2 * c + half, :, 256:384] = vstep[at, lanes]
    eb[gr] = es[gr]
    for p in y_peers:
        send(3, es.at[p], eb.at[gr], (p, gc, hd))

    whole(2, xr).wait_recv()
    uvals = jnp.zeros((64, 256), F32)
    proj = jnp.zeros((64, 512), F32)
    for f in range(4):
        part, at = xr[f], slice(256 * f, 256 * f + 256)
        uvals = uvals + nn(part, wd[0, at, :])
        proj = proj + nt(part, wh[:, at])
    hstep = jax.nn.softplus(proj[:, 256:512] + by_head([bias[0, h] for h in range(4)], (64, 256)))
    sums = segment_sums(hstep * by_head([-decay[0, h] for h in range(4)], (64, 256)), 64, 4)
    scores = dots(proj[:, 128:256], proj[:, 0:128], 4)
    i, lane = iotas((64, 256))
    mixing = jnp.where(i >= lane % 64, scores * jnp.exp(sums), 0.0)
    k, lane = iotas((256, 256))
    x_high, x_low = (
        jnp.where(k // 64 == lane // 64, jnp.concatenate([part] * 4, axis=0), jnp.zeros((), BF16))
        for part in split(hstep * uvals)
    )
    high, low = split(mixing)
    yh = nn(high, x_high) + nn(low, x_high) + nn(high, x_low)
    yh = yh + uvals * by_head([skip[h] for h in range(4)], (64, 256))
    for half in range(2):
        yhz[half] = yh[:, 128 * half : 128 * half + 128]
    mine = 8 * gr + gc
    yb[pl.ds(mine, 1), :] = yhz[core, pl.ds(8 * gc + chip, 1), :]
    for p, q in plane:
        send(4, yhz.at[lax.rem(p, 2), pl.ds(8 * q + lax.div(p, 2), 1), :], yb.at[pl.ds(mine, 1), :], (p, q, hd))

    for p in x_peers:
        send(5, columns(p), woc.at[hd], (gr, gc, p))

    whole(3, eb).wait_recv()
    ready = eb[...].reshape(128, 384)
    vdt = ready[:, 256:384]
    rates = jnp.concatenate(
        [
            jnp.broadcast_to(vdt[:, 64 * h : 64 * h + 1] * -decay[1, 2 * core + h], (128, 128))
            for h in range(2)
        ],
        axis=1,
    )
    sums = segment_sums(rates, 128, 2)
    bmat, cmat = (jnp.concatenate([ready[:, at : at + 64]] * 2, axis=1) for at in (128, 192))
    scores = dots(cmat, bmat, 2)
    i, lane = iotas((128, 256))
    high, low = split(jnp.where(i >= lane % 128, scores * jnp.exp(sums), 0.0))
    mix[:, 0:256] = high
    mix[:, 256:512] = low

    whole(0, zb).wait_send()
    whole(1, xt).wait_send()
    whole(2, xr).wait_send()
    whole(3, eb).wait_send()
    whole(4, yb).wait_send()
    whole(5, woc).wait_send()

    whole(4, yb).wait_recv()
    yh = yb[...]
    k, lane = iotas((128, 128))
    zero = jnp.zeros((), BF16)
    x_high, x_low = (
        jnp.concatenate([jnp.where(lane < 64, part, zero), jnp.where(lane >= 64, part, zero)], axis=0)
        for part in split(eb[...].reshape(128, 384)[:, 256:384] * yh)
    )
    yv = nn(mix[:, 0:256], x_high) + nn(mix[:, 256:512], x_high) + nn(mix[:, 0:256], x_low) + yh
    high, low = split(yv * yv)
    k, lane = iotas((256, 128))
    same = jnp.where((k % 128) // 64 == lane // 64, 1.0, 0.0).astype(BF16)
    meansq = nn(jnp.concatenate([high, low], axis=1), same) * (1.0 / 64.0)
    hidden = yv * lax.rsqrt(meansq + 1e-05) * eb[...].reshape(128, 384)[:, 0:128]
    hs[...] = hidden.reshape(16, 8, 128).astype(BF16)

    slot = (2 * hd + core) * 8 + chip
    hx[slot] = hs[gr]
    for p in y_peers + [gr]:
        for q in x_peers + [hd]:
            if not (p is gr and q is hd):
                send(7, hs.at[p], hx.at[slot], (p, gc, q))
    whole(5, woc).wait_recv()

    whole(7, hx).wait_recv()
    mixed = jnp.zeros((64, 256), F32)
    for f in range(4):
        part = [hx[at : at + 8].astype(F32).reshape(64, 128) for at in (16 * f, 16 * f + 8)]
        mixed = mixed + nn(jnp.concatenate(part, axis=1).astype(BF16), woc[f])
    for c in range(8):
        for half in range(2):
            ot[half, pl.ds(c, 8, stride=8), :] = mixed[8 * c : 8 * c + 8, 128 * half : 128 * half + 128]
    out[...] = jnp.concatenate([ot[0], ot[1]], axis=1).astype(BF16)
    whole(7, hx).wait_send()


def on_device(patches, w_in, w_bc, w_step, step_bias, decay_rate, skip_gain, norm_gain, w_out):
    hbm, vmem, smem = (pl.BlockSpec(memory_space=m) for m in (pltpu.HBM, pltpu.VMEM, pltpu.SMEM))
    scratch = [
        pltpu.VMEM((8, 8, 256), BF16),
        pltpu.VMEM((8, 16, 128), BF16),
        pltpu.VMEM((8, 16, 128), BF16),
        pltpu.VMEM((4, 64, 256), BF16),
        pltpu.VMEM((4, 64, 256), BF16),
        pltpu.VMEM((1024, 2, 256), BF16),
        pltpu.VMEM((2, 1024, 256), BF16),
        pltpu.VMEM((256, 1024), BF16),
        pltpu.VMEM((2, 4, 1024), BF16),
        pltpu.VMEM((512, 1024), BF16),
        pltpu.VMEM((256, 1024), BF16),
        pltpu.VMEM((4, 256, 256), BF16),
        pltpu.VMEM((1, 256), F32),
        pltpu.SMEM((2, 4), F32),
        pltpu.SMEM((2, 4), F32),
        pltpu.SMEM((4,), F32),
        pltpu.VMEM((2, 64, 128), F32),
        pltpu.VMEM((16, 8, 384), F32),
        pltpu.VMEM((16, 8, 384), F32),
        pltpu.VMEM((128, 128), F32),
        pltpu.VMEM((16, 8, 128), BF16),
        pltpu.VMEM((64, 8, 128), BF16),
        pltpu.VMEM((2, 64, 128), F32),
        pltpu.VMEM((128, 512), BF16),
        pltpu.SemaphoreType.DMA((9,)),
        pltpu.SemaphoreType.DMA((8,)),
        pltpu.SemaphoreType.DMA((8,)),
    ]
    mixed = pl.pallas_call(
        layer,
        out_shape=jax.ShapeDtypeStruct((64, 256), BF16),
        in_specs=[hbm] * 9,
        out_specs=vmem,
        scratch_shapes=scratch,
        compiler_params=pltpu.CompilerParams(
            collective_id=0, has_side_effects=True, vmem_limit_bytes=60 * 2**20
        ),
    )(
        patches,
        w_in,
        w_bc.transpose(1, 2, 0).reshape(256, 1024),
        w_step.transpose(1, 2, 0),
        step_bias,
        decay_rate,
        skip_gain,
        norm_gain.reshape(1, 256),
        w_out,
    )
    return mixed.reshape(8, 8, 256)


def solution(mesh):
    in_specs = (
        P("gr", "gc", "hd"),
        P(None, None, "hd"),
        P(),
        P(None, None, "hd"),
        P(None, "hd"),
        P(None, "hd"),
        P("hd"),
        P("hd"),
        P("hd", None),
    )
    out_specs = P("gr", "gc", "hd")
    return jax.shard_map(
        on_device, mesh=mesh, in_specs=in_specs, out_specs=out_specs, check_vma=False
    )
```

```python
import functools

import jax
import jax.numpy as jnp
from jax import lax
from jax.experimental import pallas as pl
from jax.experimental.pallas import tpu as pltpu
from jax.sharding import PartitionSpec as P

MESH = pl.DeviceIdType.MESH
F32, BF16 = jnp.float32, jnp.bfloat16
FAR_FIRST_8 = (4, 3, 5, 2, 6, 1, 7)
FAR_FIRST_4 = (2, 1, 3)


def nn(a, b):
    return lax.dot_general(a, b, (((1,), (0,)), ((), ())), preferred_element_type=F32)


def nt(a, b):
    return lax.dot_general(a, b, (((1,), (1,)), ((), ())), preferred_element_type=F32)


def split(a):
    high = a.astype(BF16)
    return high, (a - high.astype(F32)).astype(BF16)


def iotas(shape):
    return lax.broadcasted_iota(jnp.int32, shape, 0), lax.broadcasted_iota(jnp.int32, shape, 1)


def by_head(values, shape):
    lane = lax.broadcasted_iota(jnp.int32, shape, 1)
    row = jnp.full(shape, values[-1], F32)
    for h in range(len(values) - 2, -1, -1):
        row = jnp.where(lane < 64 * (h + 1), values[h], row)
    return row


def dots(c, b, copies):
    (c_high, c_low), (b_high, b_low) = split(c), split(b)
    lane = iotas(c.shape)[1]
    zero = jnp.zeros((), BF16)
    left = [jnp.where(lane < 64, c_high, c_low), jnp.where(lane < 64, c_high, zero)]
    right = jnp.concatenate([b_high, jnp.where(lane < 64, b_low, zero)], axis=1)
    return nt(jnp.concatenate(left, axis=1), jnp.concatenate([right] * copies, axis=0))


def reaches(later, earlier, rows):
    return (later >= earlier) & (later % rows == earlier % rows)


def ones_where(mask):
    return jnp.where(mask, 1.0, 0.0).astype(BF16)


def segment_sums(rates, length, heads, rows):
    k, lane = iotas((length, heads * length))
    j = lane % length
    inside = split(jnp.where(reaches(k, j, rows) & (k != j), rates, 0.0))
    i, k = iotas((length, 2 * length))
    return nn(ones_where(reaches(i, k % length, rows)), jnp.concatenate(inside, axis=0))


def sums_across(rates, before):
    k, lane = iotas((64, 256))
    j = lane % 64
    after = jnp.where(reaches(k, j, 2) & (k != j), before, 0.0)
    parts = split(jnp.concatenate([rates, after], axis=0))
    i, k = iotas((64, 256))
    return nn(ones_where((k % 128 >= 64) | reaches(i, k % 64, 2)), jnp.concatenate(parts, axis=0))


def head_blocks(x):
    k, lane = iotas((256, 256))
    zero = jnp.zeros((), BF16)
    return [
        jnp.where(k // 64 == lane // 64, jnp.concatenate([part] * 4, axis=0), zero) for part in split(x)
    ]


def mixed_by(mixing, x):
    high, low = split(mixing)
    x_high, x_low = head_blocks(x)
    return nn(high, x_high) + nn(low, x_high) + nn(high, x_low)


def layer(
    patches, w_in, w_bc, w_step, bias_in, decay_in, skip_in, gain_in, w_out, out,
    pt, zs, xr, xl, xt, wi, wd, wb, wst, wh, wv, woc, gain, bias, decay, skip,
    yhz, es, eb, yb, hs, hx, ot, mix,
    load_sem, send_sem, recv_sem, ready,
):
    gr, gc, hd = lax.axis_index("gr"), lax.axis_index("gc"), lax.axis_index("hd")
    chip, core = lax.div(gr, 2), lax.rem(gr, 2)

    side, quarter = lax.div(gc, 4), lax.rem(gc, 4)

    x_peers = [lax.rem(hd + k, 4) for k in FAR_FIRST_4]
    z_peers = [4 * side + lax.rem(quarter + k, 4) for k in FAR_FIRST_4]
    y_peers = [2 * lax.rem(chip + k, 8) + c for k in FAR_FIRST_8 for c in (core, 1 - core)]
    y_peers.append(2 * chip + 1 - core)

    barrier = pltpu.get_barrier_semaphore()
    for p in z_peers:
        pl.semaphore_signal(barrier, inc=1, device_id=(gr, p, hd), device_id_type=MESH)
    for p in y_peers:
        pl.semaphore_signal(barrier, inc=1, device_id=(p, gc, hd), device_id_type=MESH)
    for p in x_peers:
        pl.semaphore_signal(barrier, inc=1, device_id=(gr, gc, p), device_id_type=MESH)

    @pl.when(side == 0)
    def _():
        for p in range(4, 8):
            pl.semaphore_signal(barrier, inc=1, device_id=(gr, p, hd), device_id_type=MESH)

    def columns(p):
        return w_out.at[:, pl.ds(pl.multiple_of(p * 256, 256), 256)]

    loads = [
        pltpu.make_async_copy(src, dst, load_sem.at[n])
        for n, (src, dst) in enumerate(
            (
                (patches, pt),
                (w_step, wst),
                (w_bc, wb),
                (w_in, wi),
                (bias_in, bias),
                (decay_in, decay),
                (skip_in, skip),
                (gain_in, gain),
                (columns(hd), woc.at[hd]),
            )
        )
    ]
    for load in loads:
        load.start()

    def send(phase, src, dst, device):
        pltpu.make_async_remote_copy(
            src_ref=src,
            dst_ref=dst,
            send_sem=send_sem.at[phase],
            recv_sem=recv_sem.at[phase],
            device_id=device,
            device_id_type=MESH,
        ).start()

    def done(phase, part):
        return pltpu.make_async_remote_copy(
            src_ref=part,
            dst_ref=part,
            send_sem=send_sem.at[phase],
            recv_sem=recv_sem.at[phase],
            device_id=(gr, gc, x_peers[0]),
            device_id_type=MESH,
        )

    def but_one(buf):
        return buf.at[pl.ds(0, buf.shape[0] - 1)]

    def sixteen(n):
        return pl.ds(pl.multiple_of(n * 16, 16), 16)

    loads[0].wait()
    tile = pt[...].astype(F32)
    for r in range(8):
        for half in range(2):
            lanes = tile[r, :, 128 * half : 128 * half + 128]
            ot[half, pl.ds(r, 8, stride=8), :] = lanes
            yhz[half, pl.ds(16 * (r // 2) + r % 2, 8, stride=2), :] = lanes
    xt[hd] = jnp.concatenate([ot[0], ot[1]], axis=1).astype(BF16)
    zs[...] = jnp.concatenate([yhz[0], yhz[1]], axis=1).astype(BF16)
    xr[hd, sixteen(quarter), :] = zs[sixteen(quarter), :]

    pl.semaphore_wait(barrier, 21 + 4 * side)

    @pl.when(side == 1)
    def _():
        for p in range(4):
            pl.semaphore_signal(ready, inc=1, device_id=(gr, p, hd), device_id_type=MESH)

    for p in z_peers:
        send(0, zs.at[sixteen(lax.rem(p, 4)), :], xr.at[hd, sixteen(quarter), :], (gr, p, hd))
    for p in x_peers:
        send(1, xt.at[hd], xt.at[hd], (gr, gc, p))

    for load in loads[1:]:
        load.wait()

    def pairs(n, carry):
        rows = pl.ds(pl.multiple_of(n * 16, 16), 16)
        both = jnp.swapaxes(wi[rows].astype(F32), 0, 1)
        wd[:, rows, :] = both.astype(BF16)
        return carry

    lax.fori_loop(0, 64, pairs, 0)
    for n in range(4):
        wh[64 * n : 64 * n + 64, :] = wb[64 * (n // 2) : 64 * (n // 2) + 64, :]
    steps = wst[...].astype(F32)
    for h in range(4):
        wh[256 + 64 * h : 320 + 64 * h, :] = jnp.broadcast_to(steps[0, h : h + 1, :], (64, 1024)).astype(BF16)
        wv[64 * h : 64 * h + 64, :] = jnp.broadcast_to(steps[1, h : h + 1, :], (64, 1024)).astype(BF16)

    done(0, xr.at[0, pl.ds(0, 48), :]).wait_recv()
    for p in x_peers:
        send(2, xr.at[hd], xr.at[hd], (gr, gc, p))

    @pl.when(side == 0)
    def _():
        pl.semaphore_wait(ready, 4)
        for p in range(4):
            send(6, zs.at[sixteen(p), :], xl.at[hd, sixteen(quarter), :], (gr, 4 + p, hd))

    done(1, but_one(xt)).wait_recv()
    gate = jnp.zeros((64, 256), F32)
    bcv = jnp.zeros((64, 128), F32)
    raw = jnp.zeros((64, 256), F32)
    for f in range(4):
        part, at = xt[f], slice(256 * f, 256 * f + 256)
        gate = gate + nn(part, wd[1, at, :])
        bcv = bcv + nt(part, wb[128:256, at])
        raw = raw + nt(part, wv[:, at])
    vstep = jax.nn.softplus(raw + by_head([bias[1, h] for h in range(4)], (64, 256)))
    gate = jax.nn.silu(gate) * gain[...]
    for c in range(8):
        at = slice(8 * c, 8 * c + 8)
        for half in range(2):
            lanes = slice(128 * half, 128 * half + 128)
            es[2 * c + half, :, 0:128] = gate[at, lanes]
            es[2 * c + half, :, 128:256] = bcv[at, :]
            es[2 * c + half, :, 256:384] = vstep[at, lanes]
    eb[gr] = es[gr]
    for p in y_peers:
        send(3, es.at[p], eb.at[gr], (p, gc, hd))

    @pl.when(side == 1)
    def _():
        done(6, xl.at[0]).wait_recv()
        for p in x_peers:
            send(8, xl.at[hd], xl.at[hd], (gr, gc, p))

    def project(patch):
        uvals = jnp.zeros((64, 256), F32)
        proj = jnp.zeros((64, 512), F32)
        for f in range(4):
            part, at = patch[f], slice(256 * f, 256 * f + 256)
            uvals = uvals + nn(part, wd[0, at, :])
            proj = proj + nt(part, wh[:, at])
        steps = jax.nn.softplus(proj[:, 256:512] + by_head([bias[0, h] for h in range(4)], (64, 256)))
        rates = steps * by_head([-decay[0, h] for h in range(4)], (64, 256))
        return uvals, proj[:, 0:128], proj[:, 128:256], rates, steps * uvals

    done(2, but_one(xr)).wait_recv()
    uvals, bmat, cmat, rates, xin = project(xr)
    i, lane = iotas((64, 256))
    mixing = dots(cmat, bmat, 4) * jnp.exp(segment_sums(rates, 64, 4, 2))
    yh = mixed_by(jnp.where(reaches(i, lane % 64, 2), mixing, 0.0), xin)
    yh = yh + uvals * by_head([skip[h] for h in range(4)], (64, 256))
    for half in range(2):
        yhz[half] = yh[:, 128 * half : 128 * half + 128]

    @pl.when(side == 1)
    def _():
        done(8, but_one(xl)).wait_recv()
        _, b_left, _, rates_left, x_left = project(xl)
        mixing = dots(cmat, b_left, 4) * jnp.exp(sums_across(rates, rates_left))
        more = mixed_by(jnp.where(i % 2 == lane % 2, mixing, 0.0), x_left)
        for half in range(2):
            yhz[half] = yhz[half] + more[:, 128 * half : 128 * half + 128]

    def pair(n):
        return pl.ds(pl.multiple_of(n * 2, 2), 2)

    mine = 4 * gr + quarter
    for r in range(2):
        yb[pl.ds(2 * mine + r, 1), :] = yhz[core, pl.ds(2 * (8 * quarter + chip) + r, 1), :]
    for p in y_peers + [gr]:
        for q in z_peers + [gc]:
            if not (p is gr and q is gc):
                column = 8 * lax.rem(q, 4) + lax.div(p, 2)
                send(4, yhz.at[lax.rem(p, 2), pair(column), :], yb.at[pair(mine), :], (p, q, hd))

    for p in x_peers:
        send(5, columns(p), woc.at[hd], (gr, gc, p))

    done(3, but_one(eb)).wait_recv()
    ready = eb[...].reshape(128, 384)
    vdt = ready[:, 256:384]
    rates = jnp.concatenate(
        [
            jnp.broadcast_to(vdt[:, 64 * h : 64 * h + 1] * -decay[1, 2 * core + h], (128, 128))
            for h in range(2)
        ],
        axis=1,
    )
    sums = segment_sums(rates, 128, 2, 1)
    bmat, cmat = (jnp.concatenate([ready[:, at : at + 64]] * 2, axis=1) for at in (128, 192))
    scores = dots(cmat, bmat, 2)
    i, lane = iotas((128, 256))
    high, low = split(jnp.where(i >= lane % 128, scores * jnp.exp(sums), 0.0))
    mix[:, 0:256] = high
    mix[:, 256:512] = low

    done(0, xr.at[0, pl.ds(0, 48), :]).wait_send()
    done(1, but_one(xt)).wait_send()
    done(2, but_one(xr)).wait_send()
    done(3, but_one(eb)).wait_send()
    done(5, but_one(woc)).wait_send()

    @pl.when(side == 0)
    def _():
        done(6, xl.at[0]).wait_send()

    @pl.when(side == 1)
    def _():
        done(8, but_one(xl)).wait_send()

    done(4, yb.at[pl.ds(0, 126)]).wait_recv()
    yh = yb[...]
    k, lane = iotas((128, 128))
    zero = jnp.zeros((), BF16)
    x_high, x_low = (
        jnp.concatenate([jnp.where(lane < 64, part, zero), jnp.where(lane >= 64, part, zero)], axis=0)
        for part in split(eb[...].reshape(128, 384)[:, 256:384] * yh)
    )
    yv = nn(mix[:, 0:256], x_high) + nn(mix[:, 256:512], x_high) + nn(mix[:, 0:256], x_low) + yh
    high, low = split(yv * yv)
    k, lane = iotas((256, 128))
    same = jnp.where((k % 128) // 64 == lane // 64, 1.0, 0.0).astype(BF16)
    meansq = nn(jnp.concatenate([high, low], axis=1), same) * (1.0 / 64.0)
    hidden = yv * lax.rsqrt(meansq + 1e-05) * eb[...].reshape(128, 384)[:, 0:128]
    hs[...] = hidden.reshape(16, 8, 128).astype(BF16)

    slot = (2 * hd + core) * 8 + chip
    hx[slot] = hs[gr]
    for p in y_peers + [gr]:
        for q in x_peers + [hd]:
            if not (p is gr and q is hd):
                send(7, hs.at[p], hx.at[slot], (p, gc, q))
    done(4, yb.at[pl.ds(0, 126)]).wait_send()
    done(5, but_one(woc)).wait_recv()

    done(7, but_one(hx)).wait_recv()
    mixed = jnp.zeros((64, 256), F32)
    for f in range(4):
        part = [hx[at : at + 8].astype(F32).reshape(64, 128) for at in (16 * f, 16 * f + 8)]
        mixed = mixed + nn(jnp.concatenate(part, axis=1).astype(BF16), woc[f])
    for c in range(8):
        for half in range(2):
            ot[half, pl.ds(c, 8, stride=8), :] = mixed[8 * c : 8 * c + 8, 128 * half : 128 * half + 128]
    out[...] = jnp.concatenate([ot[0], ot[1]], axis=1).astype(BF16)
    done(7, but_one(hx)).wait_send()


def on_device(patches, w_in, w_bc, w_step, step_bias, decay_rate, skip_gain, norm_gain, w_out):
    hbm, vmem, smem = (pl.BlockSpec(memory_space=m) for m in (pltpu.HBM, pltpu.VMEM, pltpu.SMEM))
    scratch = [
        pltpu.VMEM((8, 8, 256), BF16),
        pltpu.VMEM((64, 256), BF16),
        pltpu.VMEM((4, 64, 256), BF16),
        pltpu.VMEM((4, 64, 256), BF16),
        pltpu.VMEM((4, 64, 256), BF16),
        pltpu.VMEM((1024, 2, 256), BF16),
        pltpu.VMEM((2, 1024, 256), BF16),
        pltpu.VMEM((256, 1024), BF16),
        pltpu.VMEM((2, 4, 1024), BF16),
        pltpu.VMEM((512, 1024), BF16),
        pltpu.VMEM((256, 1024), BF16),
        pltpu.VMEM((4, 256, 256), BF16),
        pltpu.VMEM((1, 256), F32),
        pltpu.SMEM((2, 4), F32),
        pltpu.SMEM((2, 4), F32),
        pltpu.SMEM((4,), F32),
        pltpu.VMEM((2, 64, 128), F32),
        pltpu.VMEM((16, 8, 384), F32),
        pltpu.VMEM((16, 8, 384), F32),
        pltpu.VMEM((128, 128), F32),
        pltpu.VMEM((16, 8, 128), BF16),
        pltpu.VMEM((64, 8, 128), BF16),
        pltpu.VMEM((2, 64, 128), F32),
        pltpu.VMEM((128, 512), BF16),
        pltpu.SemaphoreType.DMA((9,)),
        pltpu.SemaphoreType.DMA((9,)),
        pltpu.SemaphoreType.DMA((9,)),
        pltpu.SemaphoreType.REGULAR,
    ]
    mixed = pl.pallas_call(
        layer,
        out_shape=pltpu.VMEM((64, 256), BF16),
        in_specs=[hbm] * 9,
        out_specs=vmem,
        scratch_shapes=scratch,
        compiler_params=pltpu.CompilerParams(
            collective_id=0, has_side_effects=True, vmem_limit_bytes=60 * 2**20
        ),
    )(
        patches,
        w_in,
        w_bc.transpose(1, 2, 0).reshape(256, 1024),
        w_step.transpose(1, 2, 0),
        step_bias,
        decay_rate,
        skip_gain,
        norm_gain.reshape(1, 256),
        w_out,
    )
    return mixed.reshape(8, 8, 256)


def solution(mesh):
    in_specs = (
        P("gr", "gc", "hd"),
        P(None, None, "hd"),
        P(),
        P(None, None, "hd"),
        P(None, "hd"),
        P(None, "hd"),
        P("hd"),
        P("hd"),
        P("hd", None),
    )
    out_specs = P("gr", "gc", "hd")
    return jax.shard_map(
        on_device, mesh=mesh, in_specs=in_specs, out_specs=out_specs, check_vma=False
    )
```

```python
import functools

import jax
import jax.numpy as jnp
from jax import lax
from jax.experimental import pallas as pl
from jax.experimental.pallas import tpu as pltpu
from jax.sharding import PartitionSpec as P

MESH = pl.DeviceIdType.MESH
F32, BF16 = jnp.float32, jnp.bfloat16
FAR_FIRST_8 = (4, 3, 5, 2, 6, 1, 7)
FAR_FIRST_4 = (2, 1, 3)


def nn(a, b):
    return lax.dot_general(a, b, (((1,), (0,)), ((), ())), preferred_element_type=F32)


def nt(a, b):
    return lax.dot_general(a, b, (((1,), (1,)), ((), ())), preferred_element_type=F32)


def split(a):
    high = a.astype(BF16)
    return high, (a - high.astype(F32)).astype(BF16)


def iotas(shape):
    return lax.broadcasted_iota(jnp.int32, shape, 0), lax.broadcasted_iota(jnp.int32, shape, 1)


def by_head(values, shape):
    lane = lax.broadcasted_iota(jnp.int32, shape, 1)
    row = jnp.full(shape, values[-1], F32)
    for h in range(len(values) - 2, -1, -1):
        row = jnp.where(lane < 64 * (h + 1), values[h], row)
    return row


def dots(c, b, copies):
    (c_high, c_low), (b_high, b_low) = split(c), split(b)
    lane = iotas(c.shape)[1]
    zero = jnp.zeros((), BF16)
    left = [jnp.where(lane < 64, c_high, c_low), jnp.where(lane < 64, c_high, zero)]
    right = jnp.concatenate([b_high, jnp.where(lane < 64, b_low, zero)], axis=1)
    return nt(jnp.concatenate(left, axis=1), jnp.concatenate([right] * copies, axis=0))


def reaches(later, earlier, rows):
    return (later >= earlier) & (later % rows == earlier % rows)


def ones_where(mask):
    return jnp.where(mask, 1.0, 0.0).astype(BF16)


def segment_sums(rates, length, heads, rows):
    k, lane = iotas((length, heads * length))
    j = lane % length
    inside = split(jnp.where(reaches(k, j, rows) & (k != j), rates, 0.0))
    i, k = iotas((length, 2 * length))
    return nn(ones_where(reaches(i, k % length, rows)), jnp.concatenate(inside, axis=0))


def sums_across(rates, before):
    k, lane = iotas((64, 256))
    j = lane % 64
    after = jnp.where(reaches(k, j, 2) & (k != j), before, 0.0)
    parts = split(jnp.concatenate([rates, after], axis=0))
    i, k = iotas((64, 256))
    return nn(ones_where((k % 128 >= 64) | reaches(i, k % 64, 2)), jnp.concatenate(parts, axis=0))


def head_blocks(x):
    k, lane = iotas((256, 256))
    zero = jnp.zeros((), BF16)
    return [
        jnp.where(k // 64 == lane // 64, jnp.concatenate([part] * 4, axis=0), zero) for part in split(x)
    ]


def mixed_by(mixing, x):
    high, low = split(mixing)
    x_high, x_low = head_blocks(x)
    return nn(high, x_high) + nn(low, x_high) + nn(high, x_low)


def layer(
    patches, w_in, w_bc, w_step, bias_in, decay_in, skip_in, gain_in, w_out, out,
    pt, zs, xr, xl, xt, wi, wd, wb, wst, wh, wv, woc, gain, bias, decay, skip,
    yhz, es, eb, yb, hs, hx, ot, mix,
    load_sem, send_sem, recv_sem, ready,
):
    gr, gc, hd = lax.axis_index("gr"), lax.axis_index("gc"), lax.axis_index("hd")
    chip, core = lax.div(gr, 2), lax.rem(gr, 2)

    side, quarter = lax.div(gc, 4), lax.rem(gc, 4)

    x_peers = [lax.rem(hd + k, 4) for k in FAR_FIRST_4]
    z_peers = [4 * side + lax.rem(quarter + k, 4) for k in FAR_FIRST_4]
    y_peers = [2 * lax.rem(chip + k, 8) + c for k in FAR_FIRST_8 for c in (core, 1 - core)]
    y_peers.append(2 * chip + 1 - core)

    barrier = pltpu.get_barrier_semaphore()
    for p in z_peers:
        pl.semaphore_signal(barrier, inc=1, device_id=(gr, p, hd), device_id_type=MESH)
    for p in y_peers:
        pl.semaphore_signal(barrier, inc=1, device_id=(p, gc, hd), device_id_type=MESH)
    for p in x_peers:
        pl.semaphore_signal(barrier, inc=1, device_id=(gr, gc, p), device_id_type=MESH)

    @pl.when(side == 0)
    def _():
        for p in range(4, 8):
            pl.semaphore_signal(barrier, inc=1, device_id=(gr, p, hd), device_id_type=MESH)

    def columns(p):
        return w_out.at[:, pl.ds(pl.multiple_of(p * 256, 256), 256)]

    loads = [
        pltpu.make_async_copy(src, dst, load_sem.at[n])
        for n, (src, dst) in enumerate(
            (
                (patches, pt),
                (w_step, wst),
                (w_bc, wb),
                (w_in, wi),
                (bias_in, bias),
                (decay_in, decay),
                (skip_in, skip),
                (gain_in, gain),
                (columns(hd), woc.at[hd]),
            )
        )
    ]
    for load in loads:
        load.start()

    def send(phase, src, dst, device):
        pltpu.make_async_remote_copy(
            src_ref=src,
            dst_ref=dst,
            send_sem=send_sem.at[phase],
            recv_sem=recv_sem.at[phase],
            device_id=device,
            device_id_type=MESH,
        ).start()

    def done(phase, part):
        return pltpu.make_async_remote_copy(
            src_ref=part,
            dst_ref=part,
            send_sem=send_sem.at[phase],
            recv_sem=recv_sem.at[phase],
            device_id=(gr, gc, x_peers[0]),
            device_id_type=MESH,
        )

    def but_one(buf):
        return buf.at[pl.ds(0, buf.shape[0] - 1)]

    def sixteen(n):
        return pl.ds(pl.multiple_of(n * 16, 16), 16)

    loads[0].wait()
    tile = pt[...].astype(F32)
    for r in range(8):
        for half in range(2):
            lanes = tile[r, :, 128 * half : 128 * half + 128]
            ot[half, pl.ds(r, 8, stride=8), :] = lanes
            yhz[half, pl.ds(16 * (r // 2) + r % 2, 8, stride=2), :] = lanes
    xt[hd] = jnp.concatenate([ot[0], ot[1]], axis=1).astype(BF16)
    zs[...] = jnp.concatenate([yhz[0], yhz[1]], axis=1).astype(BF16)
    xr[hd, sixteen(quarter), :] = zs[sixteen(quarter), :]

    pl.semaphore_wait(barrier, 21 + 4 * side)

    @pl.when(side == 1)
    def _():
        for p in range(4):
            pl.semaphore_signal(ready, inc=1, device_id=(gr, p, hd), device_id_type=MESH)

    for p in z_peers:
        send(0, zs.at[sixteen(lax.rem(p, 4)), :], xr.at[hd, sixteen(quarter), :], (gr, p, hd))
    for p in x_peers:
        send(1, xt.at[hd], xt.at[hd], (gr, gc, p))

    for load in loads[1:]:
        load.wait()

    def pairs(n, carry):
        rows = pl.ds(pl.multiple_of(n * 16, 16), 16)
        both = jnp.swapaxes(wi[rows].astype(F32), 0, 1)
        wd[:, rows, :] = both.astype(BF16)
        return carry

    lax.fori_loop(0, 64, pairs, 0)
    for n in range(4):
        wh[64 * n : 64 * n + 64, :] = wb[64 * (n // 2) : 64 * (n // 2) + 64, :]
    steps = wst[...].astype(F32)
    for h in range(4):
        wh[256 + 64 * h : 320 + 64 * h, :] = jnp.broadcast_to(steps[0, h : h + 1, :], (64, 1024)).astype(BF16)
        wv[64 * h : 64 * h + 64, :] = jnp.broadcast_to(steps[1, h : h + 1, :], (64, 1024)).astype(BF16)

    done(0, xr.at[0, pl.ds(0, 48), :]).wait_recv()
    for p in x_peers:
        send(2, xr.at[hd], xr.at[hd], (gr, gc, p))

    done(1, but_one(xt)).wait_recv()
    gate = jnp.zeros((64, 256), F32)
    bcv = jnp.zeros((64, 128), F32)
    raw = jnp.zeros((64, 256), F32)
    for f in range(4):
        part, at = xt[f], slice(256 * f, 256 * f + 256)
        gate = gate + nn(part, wd[1, at, :])
        bcv = bcv + nt(part, wb[128:256, at])
        raw = raw + nt(part, wv[:, at])
    vstep = jax.nn.softplus(raw + by_head([bias[1, h] for h in range(4)], (64, 256)))
    gate = jax.nn.silu(gate) * gain[...]
    for c in range(8):
        at = slice(8 * c, 8 * c + 8)
        for half in range(2):
            lanes = slice(128 * half, 128 * half + 128)
            es[2 * c + half, :, 0:128] = gate[at, lanes]
            es[2 * c + half, :, 128:256] = bcv[at, :]
            es[2 * c + half, :, 256:384] = vstep[at, lanes]
    eb[gr] = es[gr]
    for p in y_peers:
        send(3, es.at[p], eb.at[gr], (p, gc, hd))

    @pl.when(side == 0)
    def _():
        pl.semaphore_wait(ready, 4)
        for p in range(4):
            send(6, zs.at[sixteen(p), :], xl.at[hd, sixteen(quarter), :], (gr, 4 + p, hd))

    @pl.when(side == 1)
    def _():
        done(6, xl.at[0]).wait_recv()
        for p in x_peers:
            send(8, xl.at[hd], xl.at[hd], (gr, gc, p))

    def project(patch):
        uvals = jnp.zeros((64, 256), F32)
        proj = jnp.zeros((64, 512), F32)
        for f in range(4):
            part, at = patch[f], slice(256 * f, 256 * f + 256)
            uvals = uvals + nn(part, wd[0, at, :])
            proj = proj + nt(part, wh[:, at])
        steps = jax.nn.softplus(proj[:, 256:512] + by_head([bias[0, h] for h in range(4)], (64, 256)))
        rates = steps * by_head([-decay[0, h] for h in range(4)], (64, 256))
        return uvals, proj[:, 0:128], proj[:, 128:256], rates, steps * uvals

    done(2, but_one(xr)).wait_recv()
    uvals, bmat, cmat, rates, xin = project(xr)
    i, lane = iotas((64, 256))
    mixing = dots(cmat, bmat, 4) * jnp.exp(segment_sums(rates, 64, 4, 2))
    yh = mixed_by(jnp.where(reaches(i, lane % 64, 2), mixing, 0.0), xin)
    yh = yh + uvals * by_head([skip[h] for h in range(4)], (64, 256))
    for half in range(2):
        yhz[half] = yh[:, 128 * half : 128 * half + 128]

    @pl.when(side == 1)
    def _():
        done(8, but_one(xl)).wait_recv()
        _, b_left, _, rates_left, x_left = project(xl)
        mixing = dots(cmat, b_left, 4) * jnp.exp(sums_across(rates, rates_left))
        more = mixed_by(jnp.where(i % 2 == lane % 2, mixing, 0.0), x_left)
        for half in range(2):
            yhz[half] = yhz[half] + more[:, 128 * half : 128 * half + 128]

    def pair(n):
        return pl.ds(pl.multiple_of(n * 2, 2), 2)

    mine = 4 * gr + quarter
    for r in range(2):
        yb[pl.ds(2 * mine + r, 1), :] = yhz[core, pl.ds(2 * (8 * quarter + chip) + r, 1), :]
    for p in y_peers + [gr]:
        for q in z_peers + [gc]:
            if not (p is gr and q is gc):
                column = 8 * lax.rem(q, 4) + lax.div(p, 2)
                send(4, yhz.at[lax.rem(p, 2), pair(column), :], yb.at[pair(mine), :], (p, q, hd))

    for p in x_peers:
        send(5, columns(p), woc.at[hd], (gr, gc, p))

    done(3, but_one(eb)).wait_recv()
    ready = eb[...].reshape(128, 384)
    vdt = ready[:, 256:384]
    rates = jnp.concatenate(
        [
            jnp.broadcast_to(vdt[:, 64 * h : 64 * h + 1] * -decay[1, 2 * core + h], (128, 128))
            for h in range(2)
        ],
        axis=1,
    )
    sums = segment_sums(rates, 128, 2, 1)
    bmat, cmat = (jnp.concatenate([ready[:, at : at + 64]] * 2, axis=1) for at in (128, 192))
    scores = dots(cmat, bmat, 2)
    i, lane = iotas((128, 256))
    high, low = split(jnp.where(i >= lane % 128, scores * jnp.exp(sums), 0.0))
    mix[:, 0:256] = high
    mix[:, 256:512] = low

    done(0, xr.at[0, pl.ds(0, 48), :]).wait_send()
    done(1, but_one(xt)).wait_send()
    done(2, but_one(xr)).wait_send()
    done(3, but_one(eb)).wait_send()
    done(5, but_one(woc)).wait_send()

    @pl.when(side == 0)
    def _():
        done(6, xl.at[0]).wait_send()

    @pl.when(side == 1)
    def _():
        done(8, but_one(xl)).wait_send()

    done(4, yb.at[pl.ds(0, 126)]).wait_recv()
    yh = yb[...]
    k, lane = iotas((128, 128))
    zero = jnp.zeros((), BF16)
    x_high, x_low = (
        jnp.concatenate([jnp.where(lane < 64, part, zero), jnp.where(lane >= 64, part, zero)], axis=0)
        for part in split(eb[...].reshape(128, 384)[:, 256:384] * yh)
    )
    yv = nn(mix[:, 0:256], x_high) + nn(mix[:, 256:512], x_high) + nn(mix[:, 0:256], x_low) + yh
    high, low = split(yv * yv)
    k, lane = iotas((256, 128))
    same = jnp.where((k % 128) // 64 == lane // 64, 1.0, 0.0).astype(BF16)
    meansq = nn(jnp.concatenate([high, low], axis=1), same) * (1.0 / 64.0)
    hidden = yv * lax.rsqrt(meansq + 1e-05) * eb[...].reshape(128, 384)[:, 0:128]
    hs[...] = hidden.reshape(16, 8, 128).astype(BF16)

    slot = (2 * hd + core) * 8 + chip
    hx[slot] = hs[gr]
    for p in y_peers + [gr]:
        for q in x_peers + [hd]:
            if not (p is gr and q is hd):
                send(7, hs.at[p], hx.at[slot], (p, gc, q))
    done(4, yb.at[pl.ds(0, 126)]).wait_send()
    done(5, but_one(woc)).wait_recv()

    done(7, but_one(hx)).wait_recv()
    mixed = jnp.zeros((64, 256), F32)
    for f in range(4):
        part = [hx[at : at + 8].astype(F32).reshape(64, 128) for at in (16 * f, 16 * f + 8)]
        mixed = mixed + nn(jnp.concatenate(part, axis=1).astype(BF16), woc[f])
    for c in range(8):
        for half in range(2):
            ot[half, pl.ds(c, 8, stride=8), :] = mixed[8 * c : 8 * c + 8, 128 * half : 128 * half + 128]
    out[...] = jnp.concatenate([ot[0], ot[1]], axis=1).astype(BF16)
    done(7, but_one(hx)).wait_send()


def on_device(patches, w_in, w_bc, w_step, step_bias, decay_rate, skip_gain, norm_gain, w_out):
    hbm, vmem, smem = (pl.BlockSpec(memory_space=m) for m in (pltpu.HBM, pltpu.VMEM, pltpu.SMEM))
    scratch = [
        pltpu.VMEM((8, 8, 256), BF16),
        pltpu.VMEM((64, 256), BF16),
        pltpu.VMEM((4, 64, 256), BF16),
        pltpu.VMEM((4, 64, 256), BF16),
        pltpu.VMEM((4, 64, 256), BF16),
        pltpu.VMEM((1024, 2, 256), BF16),
        pltpu.VMEM((2, 1024, 256), BF16),
        pltpu.VMEM((256, 1024), BF16),
        pltpu.VMEM((2, 4, 1024), BF16),
        pltpu.VMEM((512, 1024), BF16),
        pltpu.VMEM((256, 1024), BF16),
        pltpu.VMEM((4, 256, 256), BF16),
        pltpu.VMEM((1, 256), F32),
        pltpu.SMEM((2, 4), F32),
        pltpu.SMEM((2, 4), F32),
        pltpu.SMEM((4,), F32),
        pltpu.VMEM((2, 64, 128), F32),
        pltpu.VMEM((16, 8, 384), F32),
        pltpu.VMEM((16, 8, 384), F32),
        pltpu.VMEM((128, 128), F32),
        pltpu.VMEM((16, 8, 128), BF16),
        pltpu.VMEM((64, 8, 128), BF16),
        pltpu.VMEM((2, 64, 128), F32),
        pltpu.VMEM((128, 512), BF16),
        pltpu.SemaphoreType.DMA((9,)),
        pltpu.SemaphoreType.DMA((9,)),
        pltpu.SemaphoreType.DMA((9,)),
        pltpu.SemaphoreType.REGULAR,
    ]
    mixed = pl.pallas_call(
        layer,
        out_shape=pltpu.VMEM((64, 256), BF16),
        in_specs=[hbm] * 9,
        out_specs=vmem,
        scratch_shapes=scratch,
        compiler_params=pltpu.CompilerParams(
            collective_id=0, has_side_effects=True, vmem_limit_bytes=60 * 2**20
        ),
    )(
        patches,
        w_in,
        w_bc.transpose(1, 2, 0).reshape(256, 1024),
        w_step.transpose(1, 2, 0),
        step_bias,
        decay_rate,
        skip_gain,
        norm_gain.reshape(1, 256),
        w_out,
    )
    return mixed.reshape(8, 8, 256)


def solution(mesh):
    in_specs = (
        P("gr", "gc", "hd"),
        P(None, None, "hd"),
        P(),
        P(None, None, "hd"),
        P(None, "hd"),
        P(None, "hd"),
        P("hd"),
        P("hd"),
        P("hd", None),
    )
    out_specs = P("gr", "gc", "hd")
    return jax.shard_map(
        on_device, mesh=mesh, in_specs=in_specs, out_specs=out_specs, check_vma=False
    )
```

```python
import functools

import jax
import jax.numpy as jnp
from jax import lax
from jax.experimental import pallas as pl
from jax.experimental.pallas import tpu as pltpu
from jax.sharding import PartitionSpec as P

MESH = pl.DeviceIdType.MESH
F32, BF16 = jnp.float32, jnp.bfloat16
FAR_FIRST_8 = (4, 3, 5, 2, 6, 1, 7)
FAR_FIRST_4 = (2, 1, 3)


def nn(a, b):
    return lax.dot_general(a, b, (((1,), (0,)), ((), ())), preferred_element_type=F32)


def nt(a, b):
    return lax.dot_general(a, b, (((1,), (1,)), ((), ())), preferred_element_type=F32)


def split(a):
    high = a.astype(BF16)
    return high, (a - high.astype(F32)).astype(BF16)


def iotas(shape):
    return lax.broadcasted_iota(jnp.int32, shape, 0), lax.broadcasted_iota(jnp.int32, shape, 1)


def by_head(values, shape):
    lane = lax.broadcasted_iota(jnp.int32, shape, 1)
    row = jnp.full(shape, values[-1], F32)
    for h in range(len(values) - 2, -1, -1):
        row = jnp.where(lane < 64 * (h + 1), values[h], row)
    return row


def dots(c, b, copies):
    (c_high, c_low), (b_high, b_low) = split(c), split(b)
    lane = iotas(c.shape)[1]
    zero = jnp.zeros((), BF16)
    left = [jnp.where(lane < 64, c_high, c_low), jnp.where(lane < 64, c_high, zero)]
    right = jnp.concatenate([b_high, jnp.where(lane < 64, b_low, zero)], axis=1)
    return nt(jnp.concatenate(left, axis=1), jnp.concatenate([right] * copies, axis=0))


def reaches(later, earlier, rows):
    return (later >= earlier) & (later % rows == earlier % rows)


def ones_where(mask):
    return jnp.where(mask, 1.0, 0.0).astype(BF16)


def segment_sums(rates, length, heads, rows):
    k, lane = iotas((length, heads * length))
    j = lane % length
    inside = split(jnp.where(reaches(k, j, rows) & (k != j), rates, 0.0))
    i, k = iotas((length, 2 * length))
    return nn(ones_where(reaches(i, k % length, rows)), jnp.concatenate(inside, axis=0))


def sums_across(rates, before):
    k, lane = iotas((64, 256))
    j = lane % 64
    after = jnp.where(reaches(k, j, 2) & (k != j), before, 0.0)
    parts = split(jnp.concatenate([rates, after], axis=0))
    i, k = iotas((64, 256))
    return nn(ones_where((k % 128 >= 64) | reaches(i, k % 64, 2)), jnp.concatenate(parts, axis=0))


def head_blocks(x):
    k, lane = iotas((256, 256))
    zero = jnp.zeros((), BF16)
    return [
        jnp.where(k // 64 == lane // 64, jnp.concatenate([part] * 4, axis=0), zero) for part in split(x)
    ]


def mixed_by(mixing, x):
    high, low = split(mixing)
    x_high, x_low = head_blocks(x)
    return nn(jnp.concatenate([high, low, high], axis=1), jnp.concatenate([x_high, x_high, x_low], axis=0))


def layer(
    patches, w_in, w_bc, w_step, bias_in, decay_in, skip_in, gain_in, w_out, out,
    pt, zs, xr, xl, xt, wi, wd, wb, wst, wh, wv, woc, gain, bias, decay, skip,
    yhz, es, eb, yb, hs, hx, ot, mix,
    load_sem, send_sem, recv_sem, left_sem, ready,
):
    gr, gc, hd = lax.axis_index("gr"), lax.axis_index("gc"), lax.axis_index("hd")
    chip, core = lax.div(gr, 2), lax.rem(gr, 2)

    side, quarter = lax.div(gc, 4), lax.rem(gc, 4)

    x_peers = [lax.rem(hd + k, 4) for k in FAR_FIRST_4]
    z_peers = [4 * side + lax.rem(quarter + k, 4) for k in FAR_FIRST_4]
    y_peers = [2 * lax.rem(chip + k, 8) + c for k in FAR_FIRST_8 for c in (core, 1 - core)]
    y_peers.append(2 * chip + 1 - core)

    barrier = pltpu.get_barrier_semaphore()
    for p in z_peers:
        pl.semaphore_signal(barrier, inc=1, device_id=(gr, p, hd), device_id_type=MESH)
    for p in y_peers:
        pl.semaphore_signal(barrier, inc=1, device_id=(p, gc, hd), device_id_type=MESH)
    for p in x_peers:
        pl.semaphore_signal(barrier, inc=1, device_id=(gr, gc, p), device_id_type=MESH)

    @pl.when(side == 0)
    def _():
        for p in range(4, 8):
            pl.semaphore_signal(barrier, inc=1, device_id=(gr, p, hd), device_id_type=MESH)

    def columns(p):
        return w_out.at[:, pl.ds(pl.multiple_of(p * 256, 256), 256)]

    loads = [
        pltpu.make_async_copy(src, dst, load_sem.at[n])
        for n, (src, dst) in enumerate(
            (
                (patches, pt),
                (w_step, wst),
                (w_bc, wb),
                (w_in, wi),
                (bias_in, bias),
                (decay_in, decay),
                (skip_in, skip),
                (gain_in, gain),
                (columns(hd), woc.at[hd]),
            )
        )
    ]
    for load in loads:
        load.start()

    def send(phase, src, dst, device, arrival=None):
        pltpu.make_async_remote_copy(
            src_ref=src,
            dst_ref=dst,
            send_sem=send_sem.at[phase],
            recv_sem=recv_sem.at[phase] if arrival is None else arrival,
            device_id=device,
            device_id_type=MESH,
        ).start()

    def done(phase, part, arrival=None):
        return pltpu.make_async_remote_copy(
            src_ref=part,
            dst_ref=part,
            send_sem=send_sem.at[phase],
            recv_sem=recv_sem.at[phase] if arrival is None else arrival,
            device_id=(gr, gc, x_peers[0]),
            device_id_type=MESH,
        )

    def but_one(buf):
        return buf.at[pl.ds(0, buf.shape[0] - 1)]

    def sixteen(n):
        return pl.ds(pl.multiple_of(n * 16, 16), 16)

    loads[0].wait()
    tile = pt[...].astype(F32)
    for r in range(8):
        for half in range(2):
            lanes = tile[r, :, 128 * half : 128 * half + 128]
            ot[half, pl.ds(r, 8, stride=8), :] = lanes
            yhz[half, pl.ds(16 * (r // 2) + r % 2, 8, stride=2), :] = lanes
    xt[hd] = jnp.concatenate([ot[0], ot[1]], axis=1).astype(BF16)
    zs[...] = jnp.concatenate([yhz[0], yhz[1]], axis=1).astype(BF16)
    xr[hd, sixteen(quarter), :] = zs[sixteen(quarter), :]

    pl.semaphore_wait(barrier, 21 + 4 * side)

    @pl.when(side == 1)
    def _():
        for p in range(4):
            pl.semaphore_signal(ready, inc=1, device_id=(gr, p, hd), device_id_type=MESH)

    for p in z_peers:
        send(0, zs.at[sixteen(lax.rem(p, 4)), :], xr.at[hd, sixteen(quarter), :], (gr, p, hd))
    for p in x_peers:
        send(1, xt.at[hd], xt.at[hd], (gr, gc, p))

    for load in loads[1:]:
        load.wait()

    def pairs(n, carry):
        rows = pl.ds(pl.multiple_of(n * 16, 16), 16)
        both = jnp.swapaxes(wi[rows].astype(F32), 0, 1)
        wd[:, rows, :] = both.astype(BF16)
        return carry

    lax.fori_loop(0, 64, pairs, 0)
    for n in range(4):
        wh[64 * n : 64 * n + 64, :] = wb[64 * (n // 2) : 64 * (n // 2) + 64, :]
    steps = wst[...].astype(F32)
    for h in range(4):
        wh[256 + 64 * h : 320 + 64 * h, :] = jnp.broadcast_to(steps[0, h : h + 1, :], (64, 1024)).astype(BF16)
        wv[64 * h : 64 * h + 64, :] = jnp.broadcast_to(steps[1, h : h + 1, :], (64, 1024)).astype(BF16)

    done(0, xr.at[0, pl.ds(0, 48), :]).wait_recv()
    for p in x_peers:
        send(2, xr.at[hd], xr.at[hd], (gr, gc, p))

    done(1, but_one(xt)).wait_recv()
    features = jnp.concatenate([xt[f] for f in range(4)], axis=1)
    gate = nn(features, wd[1])
    bcv = nt(features, wb[128:256, :])
    raw = nt(features, wv[...])
    vstep = jax.nn.softplus(raw + by_head([bias[1, h] for h in range(4)], (64, 256)))
    gate = jax.nn.silu(gate) * gain[...]
    for c in range(8):
        at = slice(8 * c, 8 * c + 8)
        for half in range(2):
            lanes = slice(128 * half, 128 * half + 128)
            es[2 * c + half, :, 0:128] = gate[at, lanes]
            es[2 * c + half, :, 128:256] = bcv[at, :]
            es[2 * c + half, :, 256:384] = vstep[at, lanes]
    eb[gr] = es[gr]
    for p in y_peers:
        send(3, es.at[p], eb.at[gr], (p, gc, hd))

    @pl.when(side == 0)
    def _():
        pl.semaphore_wait(ready, 4)
        for p in range(4):
            send(6, zs.at[sixteen(p), :], xl.at[hd, sixteen(quarter), :], (gr, 4 + p, hd), left_sem.at[quarter])

    @pl.when(side == 1)
    def _():
        for k in range(4):
            n = jnp.where(quarter < 2, 3 - k, k)
            done(6, xl.at[hd, sixteen(n), :], left_sem.at[n]).wait_recv()
            for p in x_peers:
                send(8, xl.at[hd, sixteen(n), :], xl.at[hd, sixteen(n), :], (gr, gc, p))

    def project(patch):
        features = jnp.concatenate([patch[f] for f in range(4)], axis=1)
        uvals = nn(features, wd[0])
        steps = nt(features, wh[256:512, :]) + by_head([bias[0, h] for h in range(4)], (64, 256))
        steps = jax.nn.softplus(steps)
        rates = steps * by_head([-decay[0, h] for h in range(4)], (64, 256))
        return features, uvals, nt(features, wh[0:128, :]), rates, steps * uvals

    done(2, but_one(xr)).wait_recv()
    features, uvals, bmat, rates, xin = project(xr)
    cmat = nt(features, wh[128:256, :])
    i, lane = iotas((64, 256))
    mixing = dots(cmat, bmat, 4) * jnp.exp(segment_sums(rates, 64, 4, 2))
    yh = mixed_by(jnp.where(reaches(i, lane % 64, 2), mixing, 0.0), xin)
    yh = yh + uvals * by_head([skip[h] for h in range(4)], (64, 256))
    for half in range(2):
        yhz[half] = yh[:, 128 * half : 128 * half + 128]

    @pl.when(side == 1)
    def _():
        done(8, but_one(xl)).wait_recv()
        _, _, b_left, rates_left, x_left = project(xl)
        mixing = dots(cmat, b_left, 4) * jnp.exp(sums_across(rates, rates_left))
        more = mixed_by(jnp.where(i % 2 == lane % 2, mixing, 0.0), x_left)
        for half in range(2):
            yhz[half] = yhz[half] + more[:, 128 * half : 128 * half + 128]

    def pair(n):
        return pl.ds(pl.multiple_of(n * 2, 2), 2)

    mine = 4 * gr + quarter
    for r in range(2):
        yb[pl.ds(2 * mine + r, 1), :] = yhz[core, pl.ds(2 * (8 * quarter + chip) + r, 1), :]
    for p in y_peers + [gr]:
        for q in z_peers + [gc]:
            if not (p is gr and q is gc):
                column = 8 * lax.rem(q, 4) + lax.div(p, 2)
                send(4, yhz.at[lax.rem(p, 2), pair(column), :], yb.at[pair(mine), :], (p, q, hd))

    for p in x_peers:
        send(5, columns(p), woc.at[hd], (gr, gc, p))

    done(3, but_one(eb)).wait_recv()
    ready = eb[...].reshape(128, 384)
    vdt = ready[:, 256:384]
    rates = jnp.concatenate(
        [
            jnp.broadcast_to(vdt[:, 64 * h : 64 * h + 1] * -decay[1, 2 * core + h], (128, 128))
            for h in range(2)
        ],
        axis=1,
    )
    sums = segment_sums(rates, 128, 2, 1)
    bmat, cmat = (jnp.concatenate([ready[:, at : at + 64]] * 2, axis=1) for at in (128, 192))
    scores = dots(cmat, bmat, 2)
    i, lane = iotas((128, 256))
    high, low = split(jnp.where(i >= lane % 128, scores * jnp.exp(sums), 0.0))
    mix[:, 0:256] = high
    mix[:, 256:512] = low
    mix[:, 512:768] = high

    done(0, xr.at[0, pl.ds(0, 48), :]).wait_send()
    done(1, but_one(xt)).wait_send()
    done(2, but_one(xr)).wait_send()
    done(3, but_one(eb)).wait_send()
    done(5, but_one(woc)).wait_send()

    @pl.when(side == 0)
    def _():
        done(6, xl.at[0]).wait_send()

    @pl.when(side == 1)
    def _():
        done(8, but_one(xl)).wait_send()

    done(4, yb.at[pl.ds(0, 126)]).wait_recv()
    yh = yb[...]
    k, lane = iotas((128, 128))
    zero = jnp.zeros((), BF16)
    x_high, x_low = (
        jnp.concatenate([jnp.where(lane < 64, part, zero), jnp.where(lane >= 64, part, zero)], axis=0)
        for part in split(eb[...].reshape(128, 384)[:, 256:384] * yh)
    )
    yv = nn(mix[...], jnp.concatenate([x_high, x_high, x_low], axis=0)) + yh
    high, low = split(yv * yv)
    k, lane = iotas((256, 128))
    same = jnp.where((k % 128) // 64 == lane // 64, 1.0, 0.0).astype(BF16)
    meansq = nn(jnp.concatenate([high, low], axis=1), same) * (1.0 / 64.0)
    hidden = yv * lax.rsqrt(meansq + 1e-05) * eb[...].reshape(128, 384)[:, 0:128]
    hs[...] = hidden.reshape(16, 8, 128).astype(BF16)

    slot = (2 * hd + core) * 8 + chip
    hx[slot] = hs[gr]
    for p in y_peers + [gr]:
        for q in x_peers + [hd]:
            if not (p is gr and q is hd):
                send(7, hs.at[p], hx.at[slot], (p, gc, q))
    done(4, yb.at[pl.ds(0, 126)]).wait_send()
    done(5, but_one(woc)).wait_recv()

    done(7, but_one(hx)).wait_recv()
    part = [hx[8 * n : 8 * n + 8].astype(F32).reshape(64, 128).astype(BF16) for n in range(8)]
    mixed = nn(jnp.concatenate(part, axis=1), woc[...].reshape(1024, 256))
    for c in range(8):
        for half in range(2):
            ot[half, pl.ds(c, 8, stride=8), :] = mixed[8 * c : 8 * c + 8, 128 * half : 128 * half + 128]
    out[...] = jnp.concatenate([ot[0], ot[1]], axis=1).astype(BF16)
    done(7, but_one(hx)).wait_send()


def on_device(patches, w_in, w_bc, w_step, step_bias, decay_rate, skip_gain, norm_gain, w_out):
    hbm, vmem, smem = (pl.BlockSpec(memory_space=m) for m in (pltpu.HBM, pltpu.VMEM, pltpu.SMEM))
    scratch = [
        pltpu.VMEM((8, 8, 256), BF16),
        pltpu.VMEM((64, 256), BF16),
        pltpu.VMEM((4, 64, 256), BF16),
        pltpu.VMEM((4, 64, 256), BF16),
        pltpu.VMEM((4, 64, 256), BF16),
        pltpu.VMEM((1024, 2, 256), BF16),
        pltpu.VMEM((2, 1024, 256), BF16),
        pltpu.VMEM((256, 1024), BF16),
        pltpu.VMEM((2, 4, 1024), BF16),
        pltpu.VMEM((512, 1024), BF16),
        pltpu.VMEM((256, 1024), BF16),
        pltpu.VMEM((4, 256, 256), BF16),
        pltpu.VMEM((1, 256), F32),
        pltpu.SMEM((2, 4), F32),
        pltpu.SMEM((2, 4), F32),
        pltpu.SMEM((4,), F32),
        pltpu.VMEM((2, 64, 128), F32),
        pltpu.VMEM((16, 8, 384), F32),
        pltpu.VMEM((16, 8, 384), F32),
        pltpu.VMEM((128, 128), F32),
        pltpu.VMEM((16, 8, 128), BF16),
        pltpu.VMEM((64, 8, 128), BF16),
        pltpu.VMEM((2, 64, 128), F32),
        pltpu.VMEM((128, 768), BF16),
        pltpu.SemaphoreType.DMA((9,)),
        pltpu.SemaphoreType.DMA((9,)),
        pltpu.SemaphoreType.DMA((9,)),
        pltpu.SemaphoreType.DMA((4,)),
        pltpu.SemaphoreType.REGULAR,
    ]
    mixed = pl.pallas_call(
        layer,
        out_shape=pltpu.VMEM((64, 256), BF16),
        in_specs=[hbm] * 9,
        out_specs=vmem,
        scratch_shapes=scratch,
        compiler_params=pltpu.CompilerParams(
            collective_id=0, has_side_effects=True, vmem_limit_bytes=60 * 2**20
        ),
    )(
        patches,
        w_in,
        w_bc.transpose(1, 2, 0).reshape(256, 1024),
        w_step.transpose(1, 2, 0),
        step_bias,
        decay_rate,
        skip_gain,
        norm_gain.reshape(1, 256),
        w_out,
    )
    return mixed.reshape(8, 8, 256)


def solution(mesh):
    in_specs = (
        P("gr", "gc", "hd"),
        P(None, None, "hd"),
        P(),
        P(None, None, "hd"),
        P(None, "hd"),
        P(None, "hd"),
        P("hd"),
        P("hd"),
        P("hd", None),
    )
    out_specs = P("gr", "gc", "hd")
    return jax.shard_map(
        on_device, mesh=mesh, in_specs=in_specs, out_specs=out_specs, check_vma=False
    )
```

```python
import functools

import jax
import jax.numpy as jnp
from jax import lax
from jax.experimental import pallas as pl
from jax.experimental.pallas import tpu as pltpu
from jax.sharding import PartitionSpec as P

MESH = pl.DeviceIdType.MESH
F32, BF16 = jnp.float32, jnp.bfloat16
FAR_FIRST_8 = (4, 3, 5, 2, 6, 1, 7)
FAR_FIRST_4 = (2, 1, 3)


def nn(a, b):
    return lax.dot_general(a, b, (((1,), (0,)), ((), ())), preferred_element_type=F32)


def nt(a, b):
    return lax.dot_general(a, b, (((1,), (1,)), ((), ())), preferred_element_type=F32)


def split(a):
    high = a.astype(BF16)
    return high, (a - high.astype(F32)).astype(BF16)


def iotas(shape):
    return lax.broadcasted_iota(jnp.int32, shape, 0), lax.broadcasted_iota(jnp.int32, shape, 1)


def by_head(values, shape):
    lane = lax.broadcasted_iota(jnp.int32, shape, 1)
    row = jnp.full(shape, values[-1], F32)
    for h in range(len(values) - 2, -1, -1):
        row = jnp.where(lane < 64 * (h + 1), values[h], row)
    return row


def dots(c, b, copies):
    (c_high, c_low), (b_high, b_low) = split(c), split(b)
    lane = iotas(c.shape)[1]
    zero = jnp.zeros((), BF16)
    left = [jnp.where(lane < 64, c_high, c_low), jnp.where(lane < 64, c_high, zero)]
    right = jnp.concatenate([b_high, jnp.where(lane < 64, b_low, zero)], axis=1)
    return nt(jnp.concatenate(left, axis=1), jnp.concatenate([right] * copies, axis=0))


def reaches(later, earlier, rows):
    return (later >= earlier) & (later % rows == earlier % rows)


def ones_where(mask):
    return jnp.where(mask, 1.0, 0.0).astype(BF16)


def segment_sums(rates, length, heads, rows):
    k, lane = iotas((length, heads * length))
    j = lane % length
    inside = split(jnp.where(reaches(k, j, rows) & (k != j), rates, 0.0))
    i, k = iotas((length, 2 * length))
    return nn(ones_where(reaches(i, k % length, rows)), jnp.concatenate(inside, axis=0))


def sums_across(rates, before):
    k, lane = iotas((64, 256))
    j = lane % 64
    after = jnp.where(reaches(k, j, 2) & (k != j), before, 0.0)
    parts = split(jnp.concatenate([rates, after], axis=0))
    i, k = iotas((64, 256))
    return nn(ones_where((k % 128 >= 64) | reaches(i, k % 64, 2)), jnp.concatenate(parts, axis=0))


def head_blocks(x):
    k, lane = iotas((256, 256))
    zero = jnp.zeros((), BF16)
    return [
        jnp.where(k // 64 == lane // 64, jnp.concatenate([part] * 4, axis=0), zero) for part in split(x)
    ]


def mixed_by(mixing, x):
    high, low = split(mixing)
    x_high, x_low = head_blocks(x)
    return nn(jnp.concatenate([high, low, high], axis=1), jnp.concatenate([x_high, x_high, x_low], axis=0))


def layer(
    patches, w_in, w_bc, w_step, bias_in, decay_in, skip_in, gain_in, w_out, out,
    pt, zs, xr, xl, xt, wi, wd, wb, wst, wh, wv, woc, gain, bias, decay, skip,
    yhz, es, eb, gs, gb, yb, hs, hx, ot, mix,
    load_sem, send_sem, recv_sem, left_sem, ready,
):
    gr, gc, hd = lax.axis_index("gr"), lax.axis_index("gc"), lax.axis_index("hd")
    chip, core = lax.div(gr, 2), lax.rem(gr, 2)

    side, quarter = lax.div(gc, 4), lax.rem(gc, 4)

    x_peers = [lax.rem(hd + k, 4) for k in FAR_FIRST_4]
    z_peers = [4 * side + lax.rem(quarter + k, 4) for k in FAR_FIRST_4]
    y_peers = [2 * lax.rem(chip + k, 8) + c for k in FAR_FIRST_8 for c in (core, 1 - core)]
    y_peers.append(2 * chip + 1 - core)

    barrier = pltpu.get_barrier_semaphore()
    for p in y_peers:
        pl.semaphore_signal(barrier, inc=1, device_id=(p, gc, hd), device_id_type=MESH)
    for p in z_peers:
        pl.semaphore_signal(barrier, inc=1, device_id=(gr, p, hd), device_id_type=MESH)
    for p in x_peers:
        pl.semaphore_signal(barrier, inc=1, device_id=(gr, gc, p), device_id_type=MESH)

    @pl.when(side == 0)
    def _():
        for p in range(4, 8):
            pl.semaphore_signal(barrier, inc=1, device_id=(gr, p, hd), device_id_type=MESH)

    def columns(p):
        return w_out.at[:, pl.ds(pl.multiple_of(p * 256, 256), 256)]

    loads = [
        pltpu.make_async_copy(src, dst, load_sem.at[n])
        for n, (src, dst) in enumerate(
            (
                (patches, pt),
                (w_step, wst),
                (w_bc, wb),
                (w_in, wi),
                (bias_in, bias),
                (decay_in, decay),
                (skip_in, skip),
                (gain_in, gain),
                (columns(hd), woc.at[hd]),
            )
        )
    ]
    for load in loads:
        load.start()

    def send(phase, src, dst, device, arrival=None):
        pltpu.make_async_remote_copy(
            src_ref=src,
            dst_ref=dst,
            send_sem=send_sem.at[phase],
            recv_sem=recv_sem.at[phase] if arrival is None else arrival,
            device_id=device,
            device_id_type=MESH,
        ).start()

    def done(phase, part, arrival=None):
        return pltpu.make_async_remote_copy(
            src_ref=part,
            dst_ref=part,
            send_sem=send_sem.at[phase],
            recv_sem=recv_sem.at[phase] if arrival is None else arrival,
            device_id=(gr, gc, x_peers[0]),
            device_id_type=MESH,
        )

    def but_one(buf):
        return buf.at[pl.ds(0, buf.shape[0] - 1)]

    def sixteen(n):
        return pl.ds(pl.multiple_of(n * 16, 16), 16)

    loads[0].wait()
    tile = pt[...].astype(F32)
    for r in range(8):
        for half in range(2):
            lanes = tile[r, :, 128 * half : 128 * half + 128]
            ot[half, pl.ds(r, 8, stride=8), :] = lanes
            yhz[half, pl.ds(16 * (r // 2) + r % 2, 8, stride=2), :] = lanes
    xt[hd] = jnp.concatenate([ot[0], ot[1]], axis=1).astype(BF16)
    zs[...] = jnp.concatenate([yhz[0], yhz[1]], axis=1).astype(BF16)
    xr[hd, sixteen(quarter), :] = zs[sixteen(quarter), :]

    pl.semaphore_wait(barrier, 21 + 4 * side)

    @pl.when(side == 1)
    def _():
        for p in range(4):
            pl.semaphore_signal(ready, inc=1, device_id=(gr, p, hd), device_id_type=MESH)

    for p in z_peers:
        send(0, zs.at[sixteen(lax.rem(p, 4)), :], xr.at[hd, sixteen(quarter), :], (gr, p, hd))
    for p in x_peers:
        send(1, xt.at[hd], xt.at[hd], (gr, gc, p))

    for load in loads[1:]:
        load.wait()

    def pairs(n, carry):
        rows = pl.ds(pl.multiple_of(n * 16, 16), 16)
        both = jnp.swapaxes(wi[rows].astype(F32), 0, 1)
        wd[:, rows, :] = both.astype(BF16)
        return carry

    lax.fori_loop(0, 64, pairs, 0)
    for n in range(4):
        wh[64 * n : 64 * n + 64, :] = wb[64 * (n // 2) : 64 * (n // 2) + 64, :]
    steps = wst[...].astype(F32)
    for h in range(4):
        wh[256 + 64 * h : 320 + 64 * h, :] = jnp.broadcast_to(steps[0, h : h + 1, :], (64, 1024)).astype(BF16)
        wv[64 * h : 64 * h + 64, :] = jnp.broadcast_to(steps[1, h : h + 1, :], (64, 1024)).astype(BF16)

    done(0, xr.at[0, pl.ds(0, 48), :]).wait_recv()
    for p in x_peers:
        send(2, xr.at[hd], xr.at[hd], (gr, gc, p))

    done(1, but_one(xt)).wait_recv()
    features = jnp.concatenate([xt[f] for f in range(4)], axis=1)
    gate = nn(features, wd[1])
    bcv = nt(features, wb[128:256, :])
    raw = nt(features, wv[...])
    vstep = jax.nn.softplus(raw + by_head([bias[1, h] for h in range(4)], (64, 256)))
    gate = jax.nn.silu(gate) * gain[...]
    for c in range(8):
        at = slice(8 * c, 8 * c + 8)
        for half in range(2):
            lanes = slice(128 * half, 128 * half + 128)
            es[2 * c + half, :, 0:128] = bcv[at, :]
            es[2 * c + half, :, 128:256] = vstep[at, lanes]
            gs[2 * c + half] = gate[at, lanes]
    eb[gr] = es[gr]
    gb[gr] = gs[gr]
    for p in y_peers:
        send(3, es.at[p], eb.at[gr], (p, gc, hd))

    @pl.when(side == 0)
    def _():
        pl.semaphore_wait(ready, 4)
        for p in range(4):
            send(6, zs.at[sixteen(p), :], xl.at[hd, sixteen(quarter), :], (gr, 4 + p, hd), left_sem.at[quarter])

    @pl.when(side == 1)
    def _():
        for k in range(4):
            n = jnp.where(quarter < 2, 3 - k, k)
            done(6, xl.at[hd, sixteen(n), :], left_sem.at[n]).wait_recv()
            for p in x_peers:
                send(8, xl.at[hd, sixteen(n), :], xl.at[hd, sixteen(n), :], (gr, gc, p))

    def project(patch):
        features = jnp.concatenate([patch[f] for f in range(4)], axis=1)
        uvals = nn(features, wd[0])
        steps = nt(features, wh[256:512, :]) + by_head([bias[0, h] for h in range(4)], (64, 256))
        steps = jax.nn.softplus(steps)
        rates = steps * by_head([-decay[0, h] for h in range(4)], (64, 256))
        return features, uvals, nt(features, wh[0:128, :]), rates, steps * uvals

    done(2, but_one(xr)).wait_recv()
    features, uvals, bmat, rates, xin = project(xr)
    cmat = nt(features, wh[128:256, :])
    i, lane = iotas((64, 256))
    mixing = dots(cmat, bmat, 4) * jnp.exp(segment_sums(rates, 64, 4, 2))
    yh = mixed_by(jnp.where(reaches(i, lane % 64, 2), mixing, 0.0), xin)
    yh = yh + uvals * by_head([skip[h] for h in range(4)], (64, 256))
    for half in range(2):
        yhz[half] = yh[:, 128 * half : 128 * half + 128]

    @pl.when(side == 1)
    def _():
        done(8, but_one(xl)).wait_recv()
        _, _, b_left, rates_left, x_left = project(xl)
        mixing = dots(cmat, b_left, 4) * jnp.exp(sums_across(rates, rates_left))
        more = mixed_by(jnp.where(i % 2 == lane % 2, mixing, 0.0), x_left)
        for half in range(2):
            yhz[half] = yhz[half] + more[:, 128 * half : 128 * half + 128]

    def pair(n):
        return pl.ds(pl.multiple_of(n * 2, 2), 2)

    mine = 4 * gr + quarter
    for r in range(2):
        yb[pl.ds(2 * mine + r, 1), :] = yhz[core, pl.ds(2 * (8 * quarter + chip) + r, 1), :]
    for p in y_peers + [gr]:
        for q in z_peers + [gc]:
            if not (p is gr and q is gc):
                column = 8 * lax.rem(q, 4) + lax.div(p, 2)
                send(4, yhz.at[lax.rem(p, 2), pair(column), :], yb.at[pair(mine), :], (p, q, hd))

    for p in y_peers:
        send(9, gs.at[p], gb.at[gr], (p, gc, hd))

    for p in x_peers:
        send(5, columns(p), woc.at[hd], (gr, gc, p))

    done(3, but_one(eb)).wait_recv()
    ready = eb[...].reshape(128, 256)
    vdt = ready[:, 128:256]
    rates = jnp.concatenate(
        [
            jnp.broadcast_to(vdt[:, 64 * h : 64 * h + 1] * -decay[1, 2 * core + h], (128, 128))
            for h in range(2)
        ],
        axis=1,
    )
    sums = segment_sums(rates, 128, 2, 1)
    bmat, cmat = (jnp.concatenate([ready[:, at : at + 64]] * 2, axis=1) for at in (0, 64))
    scores = dots(cmat, bmat, 2)
    i, lane = iotas((128, 256))
    high, low = split(jnp.where(i >= lane % 128, scores * jnp.exp(sums), 0.0))
    mix[:, 0:256] = high
    mix[:, 256:512] = low
    mix[:, 512:768] = high

    done(0, xr.at[0, pl.ds(0, 48), :]).wait_send()
    done(1, but_one(xt)).wait_send()
    done(2, but_one(xr)).wait_send()
    done(3, but_one(eb)).wait_send()
    done(9, but_one(gb)).wait_send()
    done(5, but_one(woc)).wait_send()

    @pl.when(side == 0)
    def _():
        done(6, xl.at[0]).wait_send()

    @pl.when(side == 1)
    def _():
        done(8, but_one(xl)).wait_send()

    done(4, yb.at[pl.ds(0, 126)]).wait_recv()
    yh = yb[...]
    k, lane = iotas((128, 128))
    zero = jnp.zeros((), BF16)
    x_high, x_low = (
        jnp.concatenate([jnp.where(lane < 64, part, zero), jnp.where(lane >= 64, part, zero)], axis=0)
        for part in split(eb[...].reshape(128, 256)[:, 128:256] * yh)
    )
    yv = nn(mix[...], jnp.concatenate([x_high, x_high, x_low], axis=0)) + yh
    high, low = split(yv * yv)
    k, lane = iotas((256, 128))
    same = ones_where((k % 128) // 64 == lane // 64)
    meansq = nn(jnp.concatenate([high, low], axis=1), same) * (1.0 / 64.0)
    done(9, but_one(gb)).wait_recv()
    hidden = yv * lax.rsqrt(meansq + 1e-05) * gb[...].reshape(128, 128)
    hs[...] = hidden.reshape(16, 8, 128).astype(BF16)

    slot = (2 * hd + core) * 8 + chip
    hx[slot] = hs[gr]
    far = zip((4, 4, 3, 3, 3, 3, 2, 2, 2, 2, 1, 1, 1, 1, 0, 0), y_peers + [gr])
    holders = [(m + n, p, q) for m, p in far for n, q in zip((2, 1, 1, 0), x_peers + [hd])]
    for _, p, q in sorted(holders[:-1], key=lambda entry: -entry[0]):
        send(7, hs.at[p], hx.at[slot], (p, gc, q))
    done(4, yb.at[pl.ds(0, 126)]).wait_send()
    done(5, but_one(woc)).wait_recv()

    done(7, but_one(hx)).wait_recv()
    part = [hx[8 * n : 8 * n + 8].astype(F32).reshape(64, 128).astype(BF16) for n in range(8)]
    mixed = nn(jnp.concatenate(part, axis=1), woc[...].reshape(1024, 256))
    for c in range(8):
        for half in range(2):
            ot[half, pl.ds(c, 8, stride=8), :] = mixed[8 * c : 8 * c + 8, 128 * half : 128 * half + 128]
    out[...] = jnp.concatenate([ot[0], ot[1]], axis=1).astype(BF16)
    done(7, but_one(hx)).wait_send()


def on_device(patches, w_in, w_bc, w_step, step_bias, decay_rate, skip_gain, norm_gain, w_out):
    hbm, vmem, smem = (pl.BlockSpec(memory_space=m) for m in (pltpu.HBM, pltpu.VMEM, pltpu.SMEM))
    scratch = [
        pltpu.VMEM((8, 8, 256), BF16),
        pltpu.VMEM((64, 256), BF16),
        pltpu.VMEM((4, 64, 256), BF16),
        pltpu.VMEM((4, 64, 256), BF16),
        pltpu.VMEM((4, 64, 256), BF16),
        pltpu.VMEM((1024, 2, 256), BF16),
        pltpu.VMEM((2, 1024, 256), BF16),
        pltpu.VMEM((256, 1024), BF16),
        pltpu.VMEM((2, 4, 1024), BF16),
        pltpu.VMEM((512, 1024), BF16),
        pltpu.VMEM((256, 1024), BF16),
        pltpu.VMEM((4, 256, 256), BF16),
        pltpu.VMEM((1, 256), F32),
        pltpu.SMEM((2, 4), F32),
        pltpu.SMEM((2, 4), F32),
        pltpu.SMEM((4,), F32),
        pltpu.VMEM((2, 64, 128), F32),
        pltpu.VMEM((16, 8, 256), F32),
        pltpu.VMEM((16, 8, 256), F32),
        pltpu.VMEM((16, 8, 128), F32),
        pltpu.VMEM((16, 8, 128), F32),
        pltpu.VMEM((128, 128), F32),
        pltpu.VMEM((16, 8, 128), BF16),
        pltpu.VMEM((64, 8, 128), BF16),
        pltpu.VMEM((2, 64, 128), F32),
        pltpu.VMEM((128, 768), BF16),
        pltpu.SemaphoreType.DMA((10,)),
        pltpu.SemaphoreType.DMA((10,)),
        pltpu.SemaphoreType.DMA((10,)),
        pltpu.SemaphoreType.DMA((4,)),
        pltpu.SemaphoreType.REGULAR,
    ]
    mixed = pl.pallas_call(
        layer,
        out_shape=pltpu.VMEM((64, 256), BF16),
        in_specs=[hbm] * 9,
        out_specs=vmem,
        scratch_shapes=scratch,
        compiler_params=pltpu.CompilerParams(
            collective_id=0, has_side_effects=True, vmem_limit_bytes=60 * 2**20
        ),
    )(
        patches,
        w_in,
        w_bc.transpose(1, 2, 0).reshape(256, 1024),
        w_step.transpose(1, 2, 0),
        step_bias,
        decay_rate,
        skip_gain,
        norm_gain.reshape(1, 256),
        w_out,
    )
    return mixed.reshape(8, 8, 256)


def solution(mesh):
    in_specs = (
        P("gr", "gc", "hd"),
        P(None, None, "hd"),
        P(),
        P(None, None, "hd"),
        P(None, "hd"),
        P(None, "hd"),
        P("hd"),
        P("hd"),
        P("hd", None),
    )
    out_specs = P("gr", "gc", "hd")
    return jax.shard_map(
        on_device, mesh=mesh, in_specs=in_specs, out_specs=out_specs, check_vma=False
    )
```

```python
import functools

import jax
import jax.numpy as jnp
from jax import lax
from jax.experimental import pallas as pl
from jax.experimental.pallas import tpu as pltpu
from jax.sharding import PartitionSpec as P

MESH = pl.DeviceIdType.MESH
F32, BF16 = jnp.float32, jnp.bfloat16
FAR_FIRST_8 = (4, 3, 5, 2, 6, 1, 7)
FAR_FIRST_4 = (2, 1, 3)


def nn(a, b):
    return lax.dot_general(a, b, (((1,), (0,)), ((), ())), preferred_element_type=F32)


def nt(a, b):
    return lax.dot_general(a, b, (((1,), (1,)), ((), ())), preferred_element_type=F32)


def split(a):
    high = a.astype(BF16)
    return high, (a - high.astype(F32)).astype(BF16)


def iotas(shape):
    return lax.broadcasted_iota(jnp.int32, shape, 0), lax.broadcasted_iota(jnp.int32, shape, 1)


def by_head(values, shape):
    lane = lax.broadcasted_iota(jnp.int32, shape, 1)
    row = jnp.full(shape, values[-1], F32)
    for h in range(len(values) - 2, -1, -1):
        row = jnp.where(lane < 64 * (h + 1), values[h], row)
    return row


def dots(c, b, copies):
    (c_high, c_low), (b_high, b_low) = split(c), split(b)
    lane = iotas(c.shape)[1]
    zero = jnp.zeros((), BF16)
    left = [jnp.where(lane < 64, c_high, c_low), jnp.where(lane < 64, c_high, zero)]
    right = jnp.concatenate([b_high, jnp.where(lane < 64, b_low, zero)], axis=1)
    return nt(jnp.concatenate(left, axis=1), jnp.concatenate([right] * copies, axis=0))


def reaches(later, earlier, rows):
    return (later >= earlier) & (later % rows == earlier % rows)


def ones_where(mask):
    return jnp.where(mask, 1.0, 0.0).astype(BF16)


def segment_sums(rates, length, heads, rows):
    k, lane = iotas((length, heads * length))
    j = lane % length
    inside = split(jnp.where(reaches(k, j, rows) & (k != j), rates, 0.0))
    i, k = iotas((length, 2 * length))
    return nn(ones_where(reaches(i, k % length, rows)), jnp.concatenate(inside, axis=0))


def sums_across(rates, before):
    k, lane = iotas((64, 256))
    j = lane % 64
    after = jnp.where(reaches(k, j, 2) & (k != j), before, 0.0)
    parts = split(jnp.concatenate([rates, after], axis=0))
    i, k = iotas((64, 256))
    return nn(ones_where((k % 128 >= 64) | reaches(i, k % 64, 2)), jnp.concatenate(parts, axis=0))


def head_blocks(x):
    k, lane = iotas((256, 256))
    zero = jnp.zeros((), BF16)
    return [
        jnp.where(k // 64 == lane // 64, jnp.concatenate([part] * 4, axis=0), zero) for part in split(x)
    ]


def mixed_by(mixing, x):
    high, low = split(mixing)
    x_high, x_low = head_blocks(x)
    return nn(jnp.concatenate([high, low, high], axis=1), jnp.concatenate([x_high, x_high, x_low], axis=0))


def layer(
    patches, w_in, w_bc, w_step, bias_in, decay_in, skip_in, gain_in, w_out, out,
    pt, zs, xr, xl, xt, wi, wd, wb, wst, wh, wv, woc, gain, bias, decay, skip,
    yhz, es, eb, gs, gb, yb, hs, hx, ot, mix,
    load_sem, send_sem, recv_sem, left_sem, ready,
):
    gr, gc, hd = lax.axis_index("gr"), lax.axis_index("gc"), lax.axis_index("hd")
    chip, core = lax.div(gr, 2), lax.rem(gr, 2)

    side, quarter = lax.div(gc, 4), lax.rem(gc, 4)

    x_peers = [lax.rem(hd + k, 4) for k in FAR_FIRST_4]
    z_peers = [4 * side + lax.rem(quarter + k, 4) for k in FAR_FIRST_4]
    y_peers = [2 * lax.rem(chip + k, 8) + c for k in FAR_FIRST_8 for c in (core, 1 - core)]
    y_peers.append(2 * chip + 1 - core)

    barrier = pltpu.get_barrier_semaphore()
    for p in y_peers:
        pl.semaphore_signal(barrier, inc=1, device_id=(p, gc, hd), device_id_type=MESH)
    for p in z_peers:
        pl.semaphore_signal(barrier, inc=1, device_id=(gr, p, hd), device_id_type=MESH)
    for p in x_peers:
        pl.semaphore_signal(barrier, inc=1, device_id=(gr, gc, p), device_id_type=MESH)

    @pl.when(side == 0)
    def _():
        for p in range(4, 8):
            pl.semaphore_signal(barrier, inc=1, device_id=(gr, p, hd), device_id_type=MESH)

    def columns(p):
        return w_out.at[:, pl.ds(pl.multiple_of(p * 256, 256), 256)]

    loads = [
        pltpu.make_async_copy(src, dst, load_sem.at[n])
        for n, (src, dst) in enumerate(
            (
                (patches, pt),
                (w_step, wst),
                (w_bc, wb),
                (w_in, wi),
                (bias_in, bias),
                (decay_in, decay),
                (skip_in, skip),
                (gain_in, gain),
                (columns(hd), woc.at[hd]),
            )
        )
    ]
    for load in loads:
        load.start()

    def send(phase, src, dst, device, arrival=None):
        pltpu.make_async_remote_copy(
            src_ref=src,
            dst_ref=dst,
            send_sem=send_sem.at[phase],
            recv_sem=recv_sem.at[phase] if arrival is None else arrival,
            device_id=device,
            device_id_type=MESH,
        ).start()

    def done(phase, part, arrival=None):
        return pltpu.make_async_remote_copy(
            src_ref=part,
            dst_ref=part,
            send_sem=send_sem.at[phase],
            recv_sem=recv_sem.at[phase] if arrival is None else arrival,
            device_id=(gr, gc, x_peers[0]),
            device_id_type=MESH,
        )

    def but_one(buf):
        return buf.at[pl.ds(0, buf.shape[0] - 1)]

    def sixteen(n):
        return pl.ds(pl.multiple_of(n * 16, 16), 16)

    loads[0].wait()
    tile = pt[...].astype(F32)
    for r in range(8):
        for half in range(2):
            lanes = tile[r, :, 128 * half : 128 * half + 128]
            ot[half, pl.ds(r, 8, stride=8), :] = lanes
            yhz[half, pl.ds(16 * (r // 2) + r % 2, 8, stride=2), :] = lanes
    xt[hd] = jnp.concatenate([ot[0], ot[1]], axis=1).astype(BF16)
    zs[...] = jnp.concatenate([yhz[0], yhz[1]], axis=1).astype(BF16)
    xr[hd, sixteen(quarter), :] = zs[sixteen(quarter), :]

    pl.semaphore_wait(barrier, 21 + 4 * side)

    @pl.when(side == 1)
    def _():
        for p in range(4):
            pl.semaphore_signal(ready, inc=1, device_id=(gr, p, hd), device_id_type=MESH)

    for p in z_peers:
        send(0, zs.at[sixteen(lax.rem(p, 4)), :], xr.at[hd, sixteen(quarter), :], (gr, p, hd))
    for p in x_peers:
        send(1, xt.at[hd], xt.at[hd], (gr, gc, p))

    for load in loads[1:]:
        load.wait()

    def pairs(n, carry):
        rows = pl.ds(pl.multiple_of(n * 16, 16), 16)
        both = jnp.swapaxes(wi[rows].astype(F32), 0, 1)
        wd[:, rows, :] = both.astype(BF16)
        return carry

    lax.fori_loop(0, 64, pairs, 0)
    for n in range(4):
        wh[64 * n : 64 * n + 64, :] = wb[64 * (n // 2) : 64 * (n // 2) + 64, :]
    steps = wst[...].astype(F32)
    for h in range(4):
        wh[256 + 64 * h : 320 + 64 * h, :] = jnp.broadcast_to(steps[0, h : h + 1, :], (64, 1024)).astype(BF16)
        wv[64 * h : 64 * h + 64, :] = jnp.broadcast_to(steps[1, h : h + 1, :], (64, 1024)).astype(BF16)

    done(0, xr.at[0, pl.ds(0, 48), :]).wait_recv()
    for p in x_peers:
        send(2, xr.at[hd], xr.at[hd], (gr, gc, p))

    done(1, but_one(xt)).wait_recv()
    features = jnp.concatenate([xt[f] for f in range(4)], axis=1)
    gate = nn(features, wd[1])
    bcv = nt(features, wb[128:256, :])
    raw = nt(features, wv[...])
    vstep = jax.nn.softplus(raw + by_head([bias[1, h] for h in range(4)], (64, 256)))
    gate = jax.nn.silu(gate) * gain[...]
    for c in range(8):
        at = slice(8 * c, 8 * c + 8)
        for half in range(2):
            lanes = slice(128 * half, 128 * half + 128)
            es[2 * c + half, :, 0:128] = bcv[at, :]
            es[2 * c + half, :, 128:256] = vstep[at, lanes]
            gs[2 * c + half] = gate[at, lanes]
    eb[gr] = es[gr]
    gb[gr] = gs[gr]
    for p in y_peers:
        send(3, es.at[p], eb.at[gr], (p, gc, hd))

    @pl.when(side == 0)
    def _():
        pl.semaphore_wait(ready, 4)
        for p in range(4):
            send(6, zs.at[sixteen(p), :], xl.at[hd, sixteen(quarter), :], (gr, 4 + p, hd), left_sem.at[quarter])

    @pl.when(side == 1)
    def _():
        for k in range(4):
            n = jnp.where(quarter < 2, 3 - k, k)
            done(6, xl.at[hd, sixteen(n), :], left_sem.at[n]).wait_recv()
            for p in x_peers:
                send(8, xl.at[hd, sixteen(n), :], xl.at[hd, sixteen(n), :], (gr, gc, p))

    def terms(uvals, steps, bmat):
        steps = steps + by_head([bias[0, h] for h in range(4)], (64, 256))
        steps = jax.nn.softplus(steps)
        rates = steps * by_head([-decay[0, h] for h in range(4)], (64, 256))
        return uvals, bmat, rates, steps * uvals

    def block_products(blocks):
        at = [pl.ds(pl.multiple_of(256 * f, 256), 256) for f in blocks]
        part = jnp.concatenate([xl[f] for f in blocks], axis=1)
        return (
            nn(part, jnp.concatenate([wd[0, n, :] for n in at], axis=0)),
            nt(part, jnp.concatenate([wh[256:512, n] for n in at], axis=1)),
            nt(part, jnp.concatenate([wh[0:128, n] for n in at], axis=1)),
        )

    done(2, but_one(xr)).wait_recv()
    features = jnp.concatenate([xr[f] for f in range(4)], axis=1)
    uvals, bmat, rates, xin = terms(
        nn(features, wd[0]), nt(features, wh[256:512, :]), nt(features, wh[0:128, :])
    )
    cmat = nt(features, wh[128:256, :])
    i, lane = iotas((64, 256))
    mixing = dots(cmat, bmat, 4) * jnp.exp(segment_sums(rates, 64, 4, 2))
    yh = mixed_by(jnp.where(reaches(i, lane % 64, 2), mixing, 0.0), xin)
    yh = yh + uvals * by_head([skip[h] for h in range(4)], (64, 256))
    for half in range(2):
        yhz[half] = yh[:, 128 * half : 128 * half + 128]

    @pl.when(side == 1)
    def _():
        own = block_products([hd])
        done(8, but_one(xl)).wait_recv()
        others = block_products(x_peers)
        _, b_left, rates_left, x_left = terms(*[a + b for a, b in zip(own, others)])
        mixing = dots(cmat, b_left, 4) * jnp.exp(sums_across(rates, rates_left))
        more = mixed_by(jnp.where(i % 2 == lane % 2, mixing, 0.0), x_left)
        for half in range(2):
            yhz[half] = yhz[half] + more[:, 128 * half : 128 * half + 128]

    def pair(n):
        return pl.ds(pl.multiple_of(n * 2, 2), 2)

    mine = 4 * gr + quarter
    for r in range(2):
        yb[pl.ds(2 * mine + r, 1), :] = yhz[core, pl.ds(2 * (8 * quarter + chip) + r, 1), :]
    for p in y_peers + [gr]:
        for q in z_peers + [gc]:
            if not (p is gr and q is gc):
                column = 8 * lax.rem(q, 4) + lax.div(p, 2)
                send(4, yhz.at[lax.rem(p, 2), pair(column), :], yb.at[pair(mine), :], (p, q, hd))

    for p in y_peers:
        send(9, gs.at[p], gb.at[gr], (p, gc, hd))

    for p in x_peers:
        send(5, columns(p), woc.at[hd], (gr, gc, p))

    done(3, but_one(eb)).wait_recv()
    ready = eb[...].reshape(128, 256)
    vdt = ready[:, 128:256]
    rates = jnp.concatenate(
        [
            jnp.broadcast_to(vdt[:, 64 * h : 64 * h + 1] * -decay[1, 2 * core + h], (128, 128))
            for h in range(2)
        ],
        axis=1,
    )
    sums = segment_sums(rates, 128, 2, 1)
    bmat, cmat = (jnp.concatenate([ready[:, at : at + 64]] * 2, axis=1) for at in (0, 64))
    scores = dots(cmat, bmat, 2)
    i, lane = iotas((128, 256))
    high, low = split(jnp.where(i >= lane % 128, scores * jnp.exp(sums), 0.0))
    mix[:, 0:256] = high
    mix[:, 256:512] = low
    mix[:, 512:768] = high

    done(0, xr.at[0, pl.ds(0, 48), :]).wait_send()
    done(1, but_one(xt)).wait_send()
    done(2, but_one(xr)).wait_send()
    done(3, but_one(eb)).wait_send()
    done(9, but_one(gb)).wait_send()
    done(5, but_one(woc)).wait_send()

    @pl.when(side == 0)
    def _():
        done(6, xl.at[0]).wait_send()

    @pl.when(side == 1)
    def _():
        done(8, but_one(xl)).wait_send()

    done(4, yb.at[pl.ds(0, 126)]).wait_recv()
    yh = yb[...]
    k, lane = iotas((128, 128))
    zero = jnp.zeros((), BF16)
    x_high, x_low = (
        jnp.concatenate([jnp.where(lane < 64, part, zero), jnp.where(lane >= 64, part, zero)], axis=0)
        for part in split(eb[...].reshape(128, 256)[:, 128:256] * yh)
    )
    yv = nn(mix[...], jnp.concatenate([x_high, x_high, x_low], axis=0)) + yh
    high, low = split(yv * yv)
    k, lane = iotas((256, 128))
    same = ones_where((k % 128) // 64 == lane // 64)
    meansq = nn(jnp.concatenate([high, low], axis=1), same) * (1.0 / 64.0)
    done(9, but_one(gb)).wait_recv()
    hidden = yv * lax.rsqrt(meansq + 1e-05) * gb[...].reshape(128, 128)
    hs[...] = hidden.reshape(16, 8, 128).astype(BF16)

    slot = (2 * hd + core) * 8 + chip
    hx[slot] = hs[gr]
    far = zip((4, 4, 3, 3, 3, 3, 2, 2, 2, 2, 1, 1, 1, 1, 0, 0), y_peers + [gr])
    holders = [(m + n, p, q) for m, p in far for n, q in zip((2, 1, 1, 0), x_peers + [hd])]
    for _, p, q in sorted(holders[:-1], key=lambda entry: -entry[0]):
        send(7, hs.at[p], hx.at[slot], (p, gc, q))
    done(4, yb.at[pl.ds(0, 126)]).wait_send()
    done(5, but_one(woc)).wait_recv()

    done(7, but_one(hx)).wait_recv()
    part = [hx[8 * n : 8 * n + 8].astype(F32).reshape(64, 128).astype(BF16) for n in range(8)]
    mixed = nn(jnp.concatenate(part, axis=1), woc[...].reshape(1024, 256))
    for c in range(8):
        for half in range(2):
            ot[half, pl.ds(c, 8, stride=8), :] = mixed[8 * c : 8 * c + 8, 128 * half : 128 * half + 128]
    out[...] = jnp.concatenate([ot[0], ot[1]], axis=1).astype(BF16)
    done(7, but_one(hx)).wait_send()


def on_device(patches, w_in, w_bc, w_step, step_bias, decay_rate, skip_gain, norm_gain, w_out):
    hbm, vmem, smem = (pl.BlockSpec(memory_space=m) for m in (pltpu.HBM, pltpu.VMEM, pltpu.SMEM))
    scratch = [
        pltpu.VMEM((8, 8, 256), BF16),
        pltpu.VMEM((64, 256), BF16),
        pltpu.VMEM((4, 64, 256), BF16),
        pltpu.VMEM((4, 64, 256), BF16),
        pltpu.VMEM((4, 64, 256), BF16),
        pltpu.VMEM((1024, 2, 256), BF16),
        pltpu.VMEM((2, 1024, 256), BF16),
        pltpu.VMEM((256, 1024), BF16),
        pltpu.VMEM((2, 4, 1024), BF16),
        pltpu.VMEM((512, 1024), BF16),
        pltpu.VMEM((256, 1024), BF16),
        pltpu.VMEM((4, 256, 256), BF16),
        pltpu.VMEM((1, 256), F32),
        pltpu.SMEM((2, 4), F32),
        pltpu.SMEM((2, 4), F32),
        pltpu.SMEM((4,), F32),
        pltpu.VMEM((2, 64, 128), F32),
        pltpu.VMEM((16, 8, 256), F32),
        pltpu.VMEM((16, 8, 256), F32),
        pltpu.VMEM((16, 8, 128), F32),
        pltpu.VMEM((16, 8, 128), F32),
        pltpu.VMEM((128, 128), F32),
        pltpu.VMEM((16, 8, 128), BF16),
        pltpu.VMEM((64, 8, 128), BF16),
        pltpu.VMEM((2, 64, 128), F32),
        pltpu.VMEM((128, 768), BF16),
        pltpu.SemaphoreType.DMA((10,)),
        pltpu.SemaphoreType.DMA((10,)),
        pltpu.SemaphoreType.DMA((10,)),
        pltpu.SemaphoreType.DMA((4,)),
        pltpu.SemaphoreType.REGULAR,
    ]
    mixed = pl.pallas_call(
        layer,
        out_shape=pltpu.VMEM((64, 256), BF16),
        in_specs=[hbm] * 9,
        out_specs=vmem,
        scratch_shapes=scratch,
        compiler_params=pltpu.CompilerParams(
            collective_id=0, has_side_effects=True, vmem_limit_bytes=60 * 2**20
        ),
    )(
        patches,
        w_in,
        w_bc.transpose(1, 2, 0).reshape(256, 1024),
        w_step.transpose(1, 2, 0),
        step_bias,
        decay_rate,
        skip_gain,
        norm_gain.reshape(1, 256),
        w_out,
    )
    return mixed.reshape(8, 8, 256)


def solution(mesh):
    in_specs = (
        P("gr", "gc", "hd"),
        P(None, None, "hd"),
        P(),
        P(None, None, "hd"),
        P(None, "hd"),
        P(None, "hd"),
        P("hd"),
        P("hd"),
        P("hd", None),
    )
    out_specs = P("gr", "gc", "hd")
    return jax.shard_map(
        on_device, mesh=mesh, in_specs=in_specs, out_specs=out_specs, check_vma=False
    )
```

```python
import functools

import jax
import jax.numpy as jnp
from jax import lax
from jax.experimental import pallas as pl
from jax.experimental.pallas import tpu as pltpu
from jax.sharding import PartitionSpec as P

MESH = pl.DeviceIdType.MESH
F32, BF16 = jnp.float32, jnp.bfloat16
FAR_FIRST_8 = (4, 3, 5, 2, 6, 1, 7)
FAR_FIRST_4 = (2, 1, 3)


def nn(a, b):
    return lax.dot_general(a, b, (((1,), (0,)), ((), ())), preferred_element_type=F32)


def nt(a, b):
    return lax.dot_general(a, b, (((1,), (1,)), ((), ())), preferred_element_type=F32)


def split(a):
    high = a.astype(BF16)
    return high, (a - high.astype(F32)).astype(BF16)


def iotas(shape):
    return lax.broadcasted_iota(jnp.int32, shape, 0), lax.broadcasted_iota(jnp.int32, shape, 1)


def by_head(values, shape):
    lane = lax.broadcasted_iota(jnp.int32, shape, 1)
    row = jnp.full(shape, values[-1], F32)
    for h in range(len(values) - 2, -1, -1):
        row = jnp.where(lane < 64 * (h + 1), values[h], row)
    return row


def dots(c, b, copies):
    (c_high, c_low), (b_high, b_low) = split(c), split(b)
    lane = iotas(c.shape)[1]
    zero = jnp.zeros((), BF16)
    left = [jnp.where(lane < 64, c_high, c_low), jnp.where(lane < 64, c_high, zero)]
    right = jnp.concatenate([b_high, jnp.where(lane < 64, b_low, zero)], axis=1)
    return nt(jnp.concatenate(left, axis=1), jnp.concatenate([right] * copies, axis=0))


def reaches(later, earlier, rows):
    return (later >= earlier) & (later % rows == earlier % rows)


def ones_where(mask):
    return jnp.where(mask, 1.0, 0.0).astype(BF16)


def segment_sums(rates, length, heads, rows):
    k, lane = iotas((length, heads * length))
    j = lane % length
    inside = split(jnp.where(reaches(k, j, rows) & (k != j), rates, 0.0))
    i, k = iotas((length, 2 * length))
    return nn(ones_where(reaches(i, k % length, rows)), jnp.concatenate(inside, axis=0))


def sums_across(rates, before):
    k, lane = iotas((64, 256))
    j = lane % 64
    after = jnp.where(reaches(k, j, 2) & (k != j), before, 0.0)
    parts = split(jnp.concatenate([rates, after], axis=0))
    i, k = iotas((64, 256))
    return nn(ones_where((k % 128 >= 64) | reaches(i, k % 64, 2)), jnp.concatenate(parts, axis=0))


def head_blocks(x):
    k, lane = iotas((256, 256))
    zero = jnp.zeros((), BF16)
    return [
        jnp.where(k // 64 == lane // 64, jnp.concatenate([part] * 4, axis=0), zero) for part in split(x)
    ]


def mixed_by(mixing, x):
    high, low = split(mixing)
    x_high, x_low = head_blocks(x)
    return nn(jnp.concatenate([high, low, high], axis=1), jnp.concatenate([x_high, x_high, x_low], axis=0))


def layer(
    patches, w_in, w_bc, w_step, bias_in, decay_in, skip_in, gain_in, w_out, out,
    pt, zs, xr, xl, xt, wi, wd, wb, wst, wh, wv, woc, gain, bias, decay, skip,
    yhz, es, eb, gs, gb, yb, hs, hx, ot, mix,
    load_sem, send_sem, recv_sem, left_sem, ready,
):
    gr, gc, hd = lax.axis_index("gr"), lax.axis_index("gc"), lax.axis_index("hd")
    chip, core = lax.div(gr, 2), lax.rem(gr, 2)

    side, quarter = lax.div(gc, 4), lax.rem(gc, 4)

    x_peers = [lax.rem(hd + k, 4) for k in FAR_FIRST_4]
    z_peers = [4 * side + lax.rem(quarter + k, 4) for k in FAR_FIRST_4]
    y_peers = [2 * lax.rem(chip + k, 8) + c for k in FAR_FIRST_8 for c in (core, 1 - core)]
    y_peers.append(2 * chip + 1 - core)

    barrier = pltpu.get_barrier_semaphore()
    for p in y_peers:
        pl.semaphore_signal(barrier, inc=1, device_id=(p, gc, hd), device_id_type=MESH)
    for p in z_peers:
        pl.semaphore_signal(barrier, inc=1, device_id=(gr, p, hd), device_id_type=MESH)
    for p in x_peers:
        pl.semaphore_signal(barrier, inc=1, device_id=(gr, gc, p), device_id_type=MESH)

    @pl.when(side == 0)
    def _():
        for p in range(4, 8):
            pl.semaphore_signal(barrier, inc=1, device_id=(gr, p, hd), device_id_type=MESH)

    def columns(p):
        return w_out.at[:, pl.ds(pl.multiple_of(p * 256, 256), 256)]

    loads = [
        pltpu.make_async_copy(src, dst, load_sem.at[n])
        for n, (src, dst) in enumerate(
            (
                (patches, pt),
                (w_step, wst),
                (w_bc, wb),
                (w_in, wi),
                (bias_in, bias),
                (decay_in, decay),
                (skip_in, skip),
                (gain_in, gain),
                (columns(hd), woc.at[hd]),
            )
        )
    ]
    for load in loads:
        load.start()

    def send(phase, src, dst, device, arrival=None):
        pltpu.make_async_remote_copy(
            src_ref=src,
            dst_ref=dst,
            send_sem=send_sem.at[phase],
            recv_sem=recv_sem.at[phase] if arrival is None else arrival,
            device_id=device,
            device_id_type=MESH,
        ).start()

    def done(phase, part, arrival=None):
        return pltpu.make_async_remote_copy(
            src_ref=part,
            dst_ref=part,
            send_sem=send_sem.at[phase],
            recv_sem=recv_sem.at[phase] if arrival is None else arrival,
            device_id=(gr, gc, x_peers[0]),
            device_id_type=MESH,
        )

    def but_one(buf):
        return buf.at[pl.ds(0, buf.shape[0] - 1)]

    def sixteen(n):
        return pl.ds(pl.multiple_of(n * 16, 16), 16)

    loads[0].wait()
    tile = pt[...].astype(F32)
    for r in range(8):
        for half in range(2):
            lanes = tile[r, :, 128 * half : 128 * half + 128]
            ot[half, pl.ds(r, 8, stride=8), :] = lanes
            yhz[half, pl.ds(16 * (r // 2) + r % 2, 8, stride=2), :] = lanes
    xt[hd] = jnp.concatenate([ot[0], ot[1]], axis=1).astype(BF16)
    zs[...] = jnp.concatenate([yhz[0], yhz[1]], axis=1).astype(BF16)
    xr[hd, sixteen(quarter), :] = zs[sixteen(quarter), :]

    pl.semaphore_wait(barrier, 21 + 4 * side)

    @pl.when(side == 1)
    def _():
        for k in range(4):
            p = jnp.where(quarter < 2, k, 3 - k)
            pl.semaphore_signal(ready, inc=1, device_id=(gr, p, hd), device_id_type=MESH)

    for p in z_peers:
        send(0, zs.at[sixteen(lax.rem(p, 4)), :], xr.at[hd, sixteen(quarter), :], (gr, p, hd))
    for p in x_peers:
        send(1, xt.at[hd], xt.at[hd], (gr, gc, p))

    for load in loads[1:]:
        load.wait()

    def pairs(n, carry):
        rows = pl.ds(pl.multiple_of(n * 16, 16), 16)
        both = jnp.swapaxes(wi[rows].astype(F32), 0, 1)
        wd[:, rows, :] = both.astype(BF16)
        return carry

    lax.fori_loop(0, 64, pairs, 0)
    for n in range(4):
        wh[64 * n : 64 * n + 64, :] = wb[64 * (n // 2) : 64 * (n // 2) + 64, :]
    steps = wst[...].astype(F32)
    for h in range(4):
        wh[256 + 64 * h : 320 + 64 * h, :] = jnp.broadcast_to(steps[0, h : h + 1, :], (64, 1024)).astype(BF16)
        wv[64 * h : 64 * h + 64, :] = jnp.broadcast_to(steps[1, h : h + 1, :], (64, 1024)).astype(BF16)

    done(0, xr.at[0, pl.ds(0, 48), :]).wait_recv()
    for p in x_peers:
        send(2, xr.at[hd], xr.at[hd], (gr, gc, p))

    done(1, but_one(xt)).wait_recv()
    features = jnp.concatenate([xt[f] for f in range(4)], axis=1)
    gate = nn(features, wd[1])
    bcv = nt(features, wb[128:256, :])
    raw = nt(features, wv[...])
    vstep = jax.nn.softplus(raw + by_head([bias[1, h] for h in range(4)], (64, 256)))
    gate = jax.nn.silu(gate) * gain[...]
    for c in range(8):
        at = slice(8 * c, 8 * c + 8)
        for half in range(2):
            lanes = slice(128 * half, 128 * half + 128)
            es[2 * c + half, :, 0:128] = bcv[at, :]
            es[2 * c + half, :, 128:256] = vstep[at, lanes]
            gs[2 * c + half] = gate[at, lanes]
    eb[gr] = es[gr]
    gb[gr] = gs[gr]
    for p in y_peers:
        send(3, es.at[p], eb.at[gr], (p, gc, hd))

    @pl.when(side == 0)
    def _():
        pl.semaphore_wait(ready, 4)
        for k in range(4):
            p = jnp.where(quarter < 2, k, 3 - k)
            send(6, zs.at[sixteen(p), :], xl.at[hd, sixteen(quarter), :], (gr, 4 + p, hd), left_sem.at[quarter])

    @pl.when(side == 1)
    def _():
        for k in range(4):
            n = jnp.where(quarter < 2, 3 - k, k)
            done(6, xl.at[hd, sixteen(n), :], left_sem.at[n]).wait_recv()
            for p in x_peers:
                send(8, xl.at[hd, sixteen(n), :], xl.at[hd, sixteen(n), :], (gr, gc, p))

    def project(patch):
        features = jnp.concatenate([patch[f] for f in range(4)], axis=1)
        uvals = nn(features, wd[0])
        steps = nt(features, wh[256:512, :]) + by_head([bias[0, h] for h in range(4)], (64, 256))
        steps = jax.nn.softplus(steps)
        rates = steps * by_head([-decay[0, h] for h in range(4)], (64, 256))
        return features, uvals, nt(features, wh[0:128, :]), rates, steps * uvals

    done(2, but_one(xr)).wait_recv()
    features, uvals, bmat, rates, xin = project(xr)
    cmat = nt(features, wh[128:256, :])
    i, lane = iotas((64, 256))
    mixing = dots(cmat, bmat, 4) * jnp.exp(segment_sums(rates, 64, 4, 2))
    yh = mixed_by(jnp.where(reaches(i, lane % 64, 2), mixing, 0.0), xin)
    yh = yh + uvals * by_head([skip[h] for h in range(4)], (64, 256))
    for half in range(2):
        yhz[half] = yh[:, 128 * half : 128 * half + 128]

    @pl.when(side == 1)
    def _():
        done(8, but_one(xl)).wait_recv()
        _, _, b_left, rates_left, x_left = project(xl)
        mixing = dots(cmat, b_left, 4) * jnp.exp(sums_across(rates, rates_left))
        more = mixed_by(jnp.where(i % 2 == lane % 2, mixing, 0.0), x_left)
        for half in range(2):
            yhz[half] = yhz[half] + more[:, 128 * half : 128 * half + 128]

    def pair(n):
        return pl.ds(pl.multiple_of(n * 2, 2), 2)

    mine = 4 * gr + quarter
    for r in range(2):
        yb[pl.ds(2 * mine + r, 1), :] = yhz[core, pl.ds(2 * (8 * quarter + chip) + r, 1), :]
    for p in y_peers + [gr]:
        for q in z_peers + [gc]:
            if not (p is gr and q is gc):
                column = 8 * lax.rem(q, 4) + lax.div(p, 2)
                send(4, yhz.at[lax.rem(p, 2), pair(column), :], yb.at[pair(mine), :], (p, q, hd))

    for p in y_peers:
        send(9, gs.at[p], gb.at[gr], (p, gc, hd))

    for p in x_peers:
        send(5, columns(p), woc.at[hd], (gr, gc, p))

    done(3, but_one(eb)).wait_recv()
    ready = eb[...].reshape(128, 256)
    vdt = ready[:, 128:256]
    rates = jnp.concatenate(
        [
            jnp.broadcast_to(vdt[:, 64 * h : 64 * h + 1] * -decay[1, 2 * core + h], (128, 128))
            for h in range(2)
        ],
        axis=1,
    )
    sums = segment_sums(rates, 128, 2, 1)
    bmat, cmat = (jnp.concatenate([ready[:, at : at + 64]] * 2, axis=1) for at in (0, 64))
    scores = dots(cmat, bmat, 2)
    i, lane = iotas((128, 256))
    high, low = split(jnp.where(i >= lane % 128, scores * jnp.exp(sums), 0.0))
    mix[:, 0:256] = high
    mix[:, 256:512] = low
    mix[:, 512:768] = high

    done(0, xr.at[0, pl.ds(0, 48), :]).wait_send()
    done(1, but_one(xt)).wait_send()
    done(2, but_one(xr)).wait_send()
    done(3, but_one(eb)).wait_send()
    done(9, but_one(gb)).wait_send()
    done(5, but_one(woc)).wait_send()

    @pl.when(side == 0)
    def _():
        done(6, xl.at[0]).wait_send()

    @pl.when(side == 1)
    def _():
        done(8, but_one(xl)).wait_send()

    done(4, yb.at[pl.ds(0, 126)]).wait_recv()
    yh = yb[...]
    k, lane = iotas((128, 128))
    zero = jnp.zeros((), BF16)
    x_high, x_low = (
        jnp.concatenate([jnp.where(lane < 64, part, zero), jnp.where(lane >= 64, part, zero)], axis=0)
        for part in split(eb[...].reshape(128, 256)[:, 128:256] * yh)
    )
    yv = nn(mix[...], jnp.concatenate([x_high, x_high, x_low], axis=0)) + yh
    high, low = split(yv * yv)
    k, lane = iotas((256, 128))
    same = ones_where((k % 128) // 64 == lane // 64)
    meansq = nn(jnp.concatenate([high, low], axis=1), same) * (1.0 / 64.0)
    done(9, but_one(gb)).wait_recv()
    hidden = yv * lax.rsqrt(meansq + 1e-05) * gb[...].reshape(128, 128)
    hs[...] = hidden.reshape(16, 8, 128).astype(BF16)

    slot = (2 * hd + core) * 8 + chip
    hx[slot] = hs[gr]
    far = zip((4, 4, 3, 3, 3, 3, 2, 2, 2, 2, 1, 1, 1, 1, 0, 0), y_peers + [gr])
    holders = [(m + n, p, q) for m, p in far for n, q in zip((2, 1, 1, 0), x_peers + [hd])]
    for _, p, q in sorted(holders[:-1], key=lambda entry: -entry[0]):
        send(7, hs.at[p], hx.at[slot], (p, gc, q))
    done(4, yb.at[pl.ds(0, 126)]).wait_send()
    done(5, but_one(woc)).wait_recv()

    done(7, but_one(hx)).wait_recv()
    part = [hx[8 * n : 8 * n + 8].astype(F32).reshape(64, 128).astype(BF16) for n in range(8)]
    mixed = nn(jnp.concatenate(part, axis=1), woc[...].reshape(1024, 256))
    for c in range(8):
        for half in range(2):
            ot[half, pl.ds(c, 8, stride=8), :] = mixed[8 * c : 8 * c + 8, 128 * half : 128 * half + 128]
    out[...] = jnp.concatenate([ot[0], ot[1]], axis=1).astype(BF16)
    done(7, but_one(hx)).wait_send()


def on_device(patches, w_in, w_bc, w_step, step_bias, decay_rate, skip_gain, norm_gain, w_out):
    hbm, vmem, smem = (pl.BlockSpec(memory_space=m) for m in (pltpu.HBM, pltpu.VMEM, pltpu.SMEM))
    scratch = [
        pltpu.VMEM((8, 8, 256), BF16),
        pltpu.VMEM((64, 256), BF16),
        pltpu.VMEM((4, 64, 256), BF16),
        pltpu.VMEM((4, 64, 256), BF16),
        pltpu.VMEM((4, 64, 256), BF16),
        pltpu.VMEM((1024, 2, 256), BF16),
        pltpu.VMEM((2, 1024, 256), BF16),
        pltpu.VMEM((256, 1024), BF16),
        pltpu.VMEM((2, 4, 1024), BF16),
        pltpu.VMEM((512, 1024), BF16),
        pltpu.VMEM((256, 1024), BF16),
        pltpu.VMEM((4, 256, 256), BF16),
        pltpu.VMEM((1, 256), F32),
        pltpu.SMEM((2, 4), F32),
        pltpu.SMEM((2, 4), F32),
        pltpu.SMEM((4,), F32),
        pltpu.VMEM((2, 64, 128), F32),
        pltpu.VMEM((16, 8, 256), F32),
        pltpu.VMEM((16, 8, 256), F32),
        pltpu.VMEM((16, 8, 128), F32),
        pltpu.VMEM((16, 8, 128), F32),
        pltpu.VMEM((128, 128), F32),
        pltpu.VMEM((16, 8, 128), BF16),
        pltpu.VMEM((64, 8, 128), BF16),
        pltpu.VMEM((2, 64, 128), F32),
        pltpu.VMEM((128, 768), BF16),
        pltpu.SemaphoreType.DMA((10,)),
        pltpu.SemaphoreType.DMA((10,)),
        pltpu.SemaphoreType.DMA((10,)),
        pltpu.SemaphoreType.DMA((4,)),
        pltpu.SemaphoreType.REGULAR,
    ]
    mixed = pl.pallas_call(
        layer,
        out_shape=pltpu.VMEM((64, 256), BF16),
        in_specs=[hbm] * 9,
        out_specs=vmem,
        scratch_shapes=scratch,
        compiler_params=pltpu.CompilerParams(
            collective_id=0, has_side_effects=True, vmem_limit_bytes=60 * 2**20
        ),
    )(
        patches,
        w_in,
        w_bc.transpose(1, 2, 0).reshape(256, 1024),
        w_step.transpose(1, 2, 0),
        step_bias,
        decay_rate,
        skip_gain,
        norm_gain.reshape(1, 256),
        w_out,
    )
    return mixed.reshape(8, 8, 256)


def solution(mesh):
    in_specs = (
        P("gr", "gc", "hd"),
        P(None, None, "hd"),
        P(),
        P(None, None, "hd"),
        P(None, "hd"),
        P(None, "hd"),
        P("hd"),
        P("hd"),
        P("hd", None),
    )
    out_specs = P("gr", "gc", "hd")
    return jax.shard_map(
        on_device, mesh=mesh, in_specs=in_specs, out_specs=out_specs, check_vma=False
    )
```
